32 devices in a mesh: tm: 8 (over z, y), space: 4 (over x, core).
Axes of the slice: x: 2, y: 2, z: 4, core: 2. Of those that a mesh axis runs over, the one named last changes fastest.
Arguments:
- snapshots: bfloat16 [4096, 3, 4096], P('tm', None, 'space'), may hold values from -6 to 6
- cell_weights: float32 [4096], P('space'), may hold values from 0.25 to 4
- triads: int32 [64, 3], replicated, may hold values from 0 to 127, as said below
- owner_slots: int32 [8, 16], replicated, may hold values from -1 to 63, as said below
Outputs:
- bispectra: float32 [128, 512], P(('tm', 'space'))
The draws below stay inside these ranges and needn't reach their ends.
Inputs may be any that keep to these rules, and one draw needn't show every extreme that they name: `triads`: every row is (k, l, k + l); all three entries are below 128. `owner_slots`: every triad index stands in exactly one slot of the table; in each row the used slots come first and the others hold -1; some owner fills all 16 slots.
All inputs are finite; a program needn't handle non-finite values.
Results may differ from the reference program's by a relative error of at most 0.0076.
Values may be sent and summed in bfloat16 or wider, within the bound.
A program may use at most 64 MiB of HBM per device.

```python
import math
import jax
import jax.numpy as jnp
from jax import lax

NB = 16
NT = 256
K = 128
NSNAP = 4096
CPD = 128
NCELLS = 4096
TRI_OWN = 8
OWNERS = 8
NTRI = 64
SLOTS = 16


def draw_triads(key, part):
    draw_one = jax.random.randint(jax.random.fold_in(key, 21), (NTRI,), 0, K)
    draw_two = jax.random.randint(jax.random.fold_in(key, 22), (NTRI,), 0, K)
    folded = draw_one + draw_two >= K
    freq_one = jnp.where(folded, K - 1 - draw_one, draw_one)
    freq_two = jnp.where(folded, K - 1 - draw_two, draw_two)
    return jnp.stack([freq_one, freq_two, freq_one + freq_two], axis=1).astype(jnp.int32)


def draw_owner_slots(key, part):
    group_total = OWNERS // 4
    owner_order = jax.random.permutation(jax.random.fold_in(key, 31), OWNERS)
    shifts = jax.random.randint(jax.random.fold_in(key, 32), (group_total,), 0, TRI_OWN // 2 + 1)
    shifts = shifts.at[0].set(TRI_OWN // 2)
    pattern = jnp.array([2, 2, -2, -2], jnp.int32)
    placed = (TRI_OWN + shifts[:, None] * pattern[None, :]).reshape(OWNERS)
    owner_loads = jnp.zeros((OWNERS,), jnp.int32).at[owner_order].set(placed)
    starts = jnp.cumsum(owner_loads) - owner_loads
    triad_order = jax.random.permutation(jax.random.fold_in(key, 33), NTRI).astype(jnp.int32)
    slot_ids = jnp.arange(SLOTS, dtype=jnp.int32)
    position = jnp.clip(starts[:, None] + slot_ids[None, :], 0, NTRI - 1)
    used = slot_ids[None, :] < owner_loads[:, None]
    return jnp.where(used, triad_order[position], -1).astype(jnp.int32)


def block_levels(stream_key, shape, split, smallest, top_value):
    level = 1.0
    for dim, parts in split:
        steps = jax.random.uniform(jax.random.fold_in(jax.random.fold_in(stream_key, 6), dim), (parts,), jnp.float32, smallest / len(split), top_value / len(split))
        level = level * jnp.repeat(jnp.exp(steps), shape[dim] // parts).reshape((-1,) + (1,) * (len(shape) - 1 - dim))
    return level


def scatter_about(stream_key, extent, deviation, bound, cuts=(), kind=jnp.bfloat16):
    values = jax.random.normal(stream_key, extent, jnp.float32) * deviation
    if len(cuts) > 0:
        values = block_levels(stream_key, extent, cuts, -0.22, 0.18) * values
    return jnp.clip(values, min=-bound, max=bound).astype(kind)


def setup_inputs(seed: int = 0) -> dict:
    streams_of = jax.random.split(jax.random.key(seed), 5)
    return {
        "snapshots": scatter_about(streams_of[0], (NSNAP, 3, NCELLS), 1.0, 6.0, ((0, 8), (2, 4))),
        "cell_weights": jnp.clip(jnp.exp(math.log(4.0) - 2.7725887 * jax.random.uniform(streams_of[1], (NCELLS,), jnp.float32) ** block_levels(streams_of[1], (NCELLS,), ((0, 4),), -0.2, 0.2)), 0.25, 4.0),
        "triads": draw_triads(jax.random.fold_in(streams_of[4], 71), 0),
        "owner_slots": draw_owner_slots(jax.random.fold_in(streams_of[4], 71), 0),
    }


def spectral_table():
    sample = jnp.arange(NT, dtype=jnp.int32)
    freq_bins = jnp.arange(K, dtype=jnp.int32)
    phase_idx = freq_bins[:, None] * sample[None, :] % NT
    angles = 2.0 * math.pi / NT * phase_idx.astype(jnp.float32)
    window = 0.5 - 0.5 * jnp.cos(2.0 * math.pi / NT * sample.astype(jnp.float32))
    norm_scale = math.sqrt(8.0 / (3.0 * NT))
    real_rows = norm_scale * window[None, :] * jnp.cos(angles)
    imag_rows = -norm_scale * window[None, :] * jnp.sin(angles)
    return jnp.stack([real_rows, imag_rows]).astype(jnp.bfloat16)

def triad_terms(spectra, weight_rows, triads, triad_index):
    triad_freqs = jnp.take(triads, triad_index, axis=0)
    first_spec = jnp.take(spectra, triad_freqs[:, 0], axis=1).astype(jnp.float32)
    second_spec = jnp.take(spectra, triad_freqs[:, 1], axis=1).astype(jnp.float32)
    third_spec = jnp.take(spectra, triad_freqs[:, 2], axis=1).astype(jnp.float32)
    prod_real = (first_spec[0] * second_spec[0] - first_spec[1] * second_spec[1]) * weight_rows
    prod_imag = (first_spec[0] * second_spec[1] + first_spec[1] * second_spec[0]) * weight_rows
    product = jnp.stack([prod_real, prod_imag]).astype(jnp.bfloat16).astype(jnp.float32)
    gram = jnp.einsum('rtbc,stdc->trbsd', product, third_spec)
    bis_real = gram[:, 0, :, 0, :] + gram[:, 1, :, 1, :]
    bis_imag = gram[:, 0, :, 1, :] - gram[:, 1, :, 0, :]
    return jnp.stack([bis_real, bis_imag], axis=1).reshape(triad_index.shape[0], 2 * NB * NB)

def reference(snapshots, cell_weights, triads, owner_slots):
    dft_table = spectral_table().astype(jnp.float32)
    weight_scale = 1.0 / math.sqrt(3.0 * NCELLS)
    all_triads = jnp.arange(NTRI, dtype=jnp.int32)

    def accumulate(carry, group_index):
        first_cell = (group_index * CPD).astype(jnp.int32)
        local_snap = lax.dynamic_slice_in_dim(snapshots, first_cell, CPD, 2)
        local_w = lax.dynamic_slice_in_dim(cell_weights, first_cell, CPD, 0) * weight_scale
        blocks = local_snap.reshape(NB, NT, 3 * CPD).astype(jnp.float32)
        spectra = jnp.einsum('rkn,bnc->rkbc', dft_table, blocks).astype(jnp.bfloat16)
        weight_rows = jnp.tile(local_w, 3)
        return (carry + triad_terms(spectra, weight_rows, triads, all_triads), None)
    start_sums = jnp.zeros((NTRI, 2 * NB * NB), jnp.float32)
    triad_sums, unused_out = lax.scan(accumulate, start_sums, jnp.arange(NCELLS // CPD, dtype=jnp.int32))
    flat_slots = owner_slots.reshape(-1)
    filled = (flat_slots >= 0).astype(jnp.float32)
    chosen = jnp.take(triad_sums, jnp.maximum(flat_slots, 0).astype(jnp.int32), axis=0)
    return chosen * filled[:, None]
```

```python
import functools
import math

import jax
import jax.numpy as jnp
import ml_dtypes
import numpy as np
from jax import lax
from jax.experimental import pallas as pl
from jax.experimental.pallas import tpu as pltpu
from jax.sharding import PartitionSpec as P

NB = 16
NT = 256
K = 128
GROUP = 8
LANES = 128
MESH = pl.DeviceIdType.MESH


def spectral_table():
    sample = np.arange(NT)
    freq_bins = np.arange(K)
    angles = 2.0 * math.pi / NT * (freq_bins[:, None] * sample[None, :] % NT)
    window = 0.5 - 0.5 * np.cos(2.0 * math.pi / NT * sample)
    scale = math.sqrt(8.0 / (3.0 * NT))
    rows = np.stack(
        [scale * window * np.cos(angles), -scale * window * np.sin(angles)], axis=1
    )
    return rows.reshape(2 * K, NT).astype(np.float32).astype(ml_dtypes.bfloat16)


def kernel(
    n,
    ns,
    weight_scale,
    snap,
    table,
    weights,
    freqs,
    out,
    recv,
    rows,
    spec,
    narrow,
    acc,
    part,
    summed,
    last,
    send_sem,
    recv_sem,
    own_sem,
    send1,
    recv1,
    send2,
    recv2,
):
    comps, times = snap.shape[0], snap.shape[1]
    me = lax.axis_index("tm")
    col = lax.axis_index("space")

    barrier = pltpu.get_barrier_semaphore()

    def greet_tm(off, carry):
        pl.semaphore_signal(
            barrier, inc=1, device_id=(lax.rem(me + off, n), col), device_id_type=MESH
        )
        return carry

    lax.fori_loop(1, n, greet_tm, 0)
    for off in range(1, ns):
        pl.semaphore_signal(
            barrier, inc=1, device_id=(me, lax.rem(col + off, ns)), device_id_type=MESH
        )
    pl.semaphore_wait(barrier, n - 1 + ns - 1)

    def exchange(c, off):
        peer = lax.rem(me + off, n)
        return pltpu.make_async_remote_copy(
            src_ref=snap.at[c, :, pl.ds(pl.multiple_of(peer * LANES, LANES), LANES)],
            dst_ref=recv.at[c, pl.ds(pl.multiple_of(me * times, 16), times), :],
            send_sem=send_sem.at[c, off],
            recv_sem=recv_sem.at[c, off],
            device_id=(peer, col),
            device_id_type=MESH,
        )

    def own(c):
        return pltpu.make_async_copy(
            snap.at[c, :, pl.ds(pl.multiple_of(me * LANES, LANES), LANES)],
            recv.at[c, pl.ds(pl.multiple_of(me * times, 16), times), :],
            own_sem.at[c],
        )

    for c in range(comps):

        def begin(off, carry, c=c):
            exchange(c, off).start()
            return carry

        lax.fori_loop(1, n, begin, 0)
        own(c).start()

    w_row = weights[pl.ds(me, 1), :] * weight_scale
    lane = lax.broadcasted_iota(jnp.int32, (2 * NB, 2 * LANES), 1)
    lane_group = lax.rem(lane, LANES) // NB
    low = lax.broadcasted_iota(jnp.int32, (NB, LANES), 1) < LANES // 2
    groups = freqs.shape[1] // GROUP
    per_owner = groups // n

    def dft(c, b):
        x = recv[c, pl.ds(pl.multiple_of(b * NT, NT), NT), :]
        y = jnp.dot(table[...], x, preferred_element_type=jnp.float32)
        rows[pl.ds(b, 2 * K, stride=NB), :] = y

    def regroup(k, carry):
        both = rows[pl.ds(pl.multiple_of(k * 2 * NB, 2 * NB), 2 * NB), :].astype(jnp.bfloat16)
        narrow[k] = both
        spec[k] = both.astype(jnp.float32)
        return carry

    def gram_group(c, g):
        owner = g // per_owner
        half = lax.rem(g, per_owner)
        prods, c_re, c_im = [], [], []
        for s in range(GROUP):
            place = g * GROUP + s
            a = spec[freqs[0, place]]
            b2 = spec[freqs[1, place]]
            c2 = narrow[freqs[2, place]]
            re = (a[:NB] * b2[:NB] - a[NB:] * b2[NB:]) * w_row
            im = (a[:NB] * b2[NB:] + a[NB:] * b2[:NB]) * w_row
            prods += [re.astype(jnp.bfloat16), im.astype(jnp.bfloat16)]
            c_re.append(c2[:NB])
            c_im.append(c2[NB:])
        left = jnp.concatenate(prods, axis=0)
        right = jnp.concatenate(c_re + c_im, axis=0)
        gram = lax.dot_general(
            left, right, (((1,), (1,)), ((), ())), preferred_element_type=jnp.float32
        )
        diag = gram[: 2 * NB]
        for s in range(1, GROUP):
            diag = jnp.where(lane_group == s, gram[2 * NB * s : 2 * NB * (s + 1)], diag)
        real = diag[:NB, :LANES] + diag[NB:, LANES:]
        imag = diag[:NB, LANES:] - diag[NB:, :LANES]
        half_turn = LANES // 2
        first = jnp.where(low, real, pltpu.roll(imag, half_turn, 1))
        second = jnp.where(low, pltpu.roll(real, half_turn, 1), imag)
        if c == 0:
            acc[2 * half, owner] = first
            acc[2 * half + 1, owner] = second
        else:
            acc[2 * half, owner] += first
            acc[2 * half + 1, owner] += second

    for c in range(comps):
        own(c).wait()
        if times % NT == 0:

            def transform(i, carry, c=c):
                dft(c, me * (times // NT) + i)
                return carry

            lax.fori_loop(0, times // NT, transform, 0)

            def arrive(off, carry, c=c):
                exchange(c, off).wait_recv()
                src = lax.rem(me - off + n, n)
                for i in range(times // NT):
                    dft(c, src * (times // NT) + i)
                return carry

            lax.fori_loop(1, n, arrive, 0)
        else:

            def arrive(off, carry, c=c):
                exchange(c, off).wait_recv()
                return carry

            lax.fori_loop(1, n, arrive, 0)

            def transform(b, carry, c=c):
                dft(c, b)
                return carry

            lax.fori_loop(0, NB, transform, 0)

        lax.fori_loop(0, K, regroup, 0, unroll=4)

        def grams(g, carry, c=c):
            gram_group(c, g)
            return carry

        lax.fori_loop(0, groups, grams, 0)

    def across(off):
        peer = lax.rem(col + off, ns)
        return pltpu.make_async_remote_copy(
            src_ref=acc.at[peer],
            dst_ref=part.at[off - 1],
            send_sem=send1.at[off - 1],
            recv_sem=recv1.at[off - 1],
            device_id=(me, peer),
            device_id_type=MESH,
        )

    for off in range(1, ns):
        across(off).start()
    for off in range(1, ns):
        across(off).wait_recv()
    total = acc[col]
    for off in range(1, ns):
        total = total + part[off - 1]
    summed[...] = total

    def along(off):
        peer = lax.rem(me + off, n)
        return pltpu.make_async_remote_copy(
            src_ref=summed.at[peer],
            dst_ref=last.at[off],
            send_sem=send2.at[off],
            recv_sem=recv2.at[off],
            device_id=(peer, col),
            device_id_type=MESH,
        )

    def begin2(off, carry):
        along(off).start()
        return carry

    lax.fori_loop(1, n, begin2, 0)

    def add2(off, total):
        along(off).wait_recv()
        return total + last[off]

    out[...] = lax.fori_loop(1, n, add2, summed[me])

    for off in range(1, ns):
        across(off).wait_send()

    def drain(off, carry):
        for c in range(comps):
            exchange(c, off).wait_send()
        along(off).wait_send()
        return carry

    lax.fori_loop(1, n, drain, 0)


def lean_kernel(
    n,
    ns,
    bins,
    weight_scale,
    snap,
    table,
    weights,
    triads,
    slots,
    out,
    series,
    tab,
    dft,
    pick,
    stage,
    recv,
    looked,
    prod,
    third,
    acc,
    tiles,
    part,
    summed,
    last,
    load_sem,
    send_sem,
    recv_sem,
    send1,
    recv1,
    send2,
    recv2,
):
    comps, times, cells = series.shape
    blocks = times // NT
    count = triads.shape[1]
    owners, per_owner = slots.shape
    total_slots = owners * per_owner
    groups = total_slots // GROUP
    halves = per_owner // GROUP
    me = lax.axis_index("tm")
    col = lax.axis_index("space")
    f32, bf16 = jnp.float32, jnp.bfloat16

    def iota(shape, axis):
        return lax.broadcasted_iota(jnp.int32, shape, axis)

    fetch_table = pltpu.make_async_copy(table, tab, load_sem.at[comps])
    fetch_table.start()

    def fetch(c):
        return pltpu.make_async_copy(snap.at[c], series.at[c], load_sem.at[c])

    for c in range(comps):
        fetch(c).start()

    barrier = pltpu.get_barrier_semaphore()

    def greet(off, carry):
        pl.semaphore_signal(
            barrier, inc=1, device_id=(lax.rem(me + off, n), col), device_id_type=MESH
        )
        return carry

    lax.fori_loop(1, n, greet, 0)
    for off in range(1, ns):
        pl.semaphore_signal(
            barrier, inc=1, device_id=(me, lax.rem(col + off, ns)), device_id_type=MESH
        )

    freq = iota((K, count), 0)
    hit = (
        (freq == triads[0:1, :]) | (freq == triads[1:2, :]) | (freq == triads[2:3, :])
    )
    used = jnp.max(jnp.where(hit, 1.0, 0.0), axis=1, keepdims=True)
    used = jnp.broadcast_to(used, (K, K))
    column = iota((K, K), 1)
    below = jnp.where(column < iota((K, K), 0), 1.0, 0.0)
    rank = jnp.dot(below.astype(bf16), used.astype(bf16), preferred_element_type=f32)
    place = jnp.where((rank == column.astype(f32)) & (used > 0.0), 1.0, 0.0)
    chosen = place.T[:bins].astype(bf16)
    fetch_table.wait()
    dft[...] = jnp.concatenate(
        [jnp.dot(chosen, tab[r], preferred_element_type=f32) for r in range(2)], axis=0
    ).astype(bf16)

    def transform(c):
        fetch(c).wait()

        def step(p, carry):
            for b in range(blocks):
                y = jnp.dot(
                    dft[...],
                    series[
                        c,
                        b * NT : (b + 1) * NT,
                        pl.ds(pl.multiple_of(p * 2 * LANES, 2 * LANES), 2 * LANES),
                    ],
                    preferred_element_type=f32,
                ).astype(bf16)
                rows = pl.ds(b * 2 * bins, 2 * bins)
                stage[c, 2 * p, rows, :] = y[:, :LANES]
                stage[c, 2 * p + 1, rows, :] = y[:, LANES:]
            return carry

        lax.fori_loop(0, n // 2, step, 0)

    def exchange(c, off):
        peer = lax.rem(me + off, n)
        return pltpu.make_async_remote_copy(
            src_ref=stage.at[c, peer],
            dst_ref=recv.at[c, me],
            send_sem=send_sem.at[c, off],
            recv_sem=recv_sem.at[c, off],
            device_id=(peer, col),
            device_id_type=MESH,
        )

    transform(0)
    pl.semaphore_wait(barrier, n - 1 + ns - 1)
    for c in range(comps):
        if c > 0:
            transform(c)

        def begin(off, carry, c=c):
            exchange(c, off).start()
            return carry

        lax.fori_loop(1, n, begin, 0)

    wide = (owners, total_slots)
    spread = jnp.where(
        lax.rem(iota((per_owner, total_slots), 1), per_owner)
        == iota((per_owner, total_slots), 0),
        1.0,
        0.0,
    )
    tiled = jnp.dot(
        slots[...].astype(f32).astype(bf16),
        spread.astype(bf16),
        preferred_element_type=f32,
    )
    own_row = iota(wide, 1) // per_owner == iota(wide, 0)
    slot_triad = jnp.sum(jnp.where(own_row, tiled, 0.0), axis=0, keepdims=True)
    holds = jnp.where(
        iota((count, total_slots), 0).astype(f32) == slot_triad, 1.0, 0.0
    ).astype(bf16)
    slot_freq = jnp.dot(
        (triads[...] + 1).astype(f32).astype(bf16), holds, preferred_element_type=f32
    )
    for role in range(3):
        named = jnp.where(
            iota((K, total_slots), 0).astype(f32) + 1.0 == slot_freq[role : role + 1, :],
            1.0,
            0.0,
        )
        chosen_all = jnp.dot(
            place.T.astype(bf16), named.astype(bf16), preferred_element_type=f32
        )
        pick[role * total_slots : (role + 1) * total_slots, :] = chosen_all.T[
            :, :bins
        ].astype(bf16)

    w_row = weights[pl.ds(me, 1), :] * weight_scale

    def look_up(c, src, ref):
        for pair in range(blocks // 2):
            sides = []
            for b in (2 * pair, 2 * pair + 1):
                both = ref[c, src, b * 2 * bins : (b + 1) * 2 * bins, :]
                if bins % 16 != 0:
                    both = both.astype(f32)
                sides += [both[:bins], both[bins:]]
            looked[...] = jnp.dot(
                pick[...],
                jnp.concatenate(sides, axis=1).astype(bf16),
                preferred_element_type=f32,
            )
            first = src * (blocks * GROUP) + pair * 2 * GROUP
            at = pl.ds(pl.multiple_of(first, 2 * GROUP), 2 * GROUP)
            at_imag = pl.ds(pl.multiple_of(NB * GROUP + first, 2 * GROUP), 2 * GROUP)

            def group(g, carry):
                def tile(role, q):
                    row = pl.multiple_of(role * total_slots + g * GROUP, GROUP)
                    return looked[pl.ds(row, GROUP), q * LANES : (q + 1) * LANES]

                re, im, c_re, c_im = [], [], [], []
                for b in range(2):
                    ar, ai = tile(0, 2 * b), tile(0, 2 * b + 1)
                    br, bi = tile(1, 2 * b), tile(1, 2 * b + 1)
                    re.append((ar * br - ai * bi) * w_row)
                    im.append((ar * bi + ai * br) * w_row)
                    c_re.append(tile(2, 2 * b))
                    c_im.append(tile(2, 2 * b + 1))
                re, im, c_re, c_im = (
                    jnp.concatenate(v, axis=0) for v in (re, im, c_re, c_im)
                )
                prod[g, at, :LANES] = re.astype(bf16)
                prod[g, at, LANES:] = im.astype(bf16)
                third[g, at, :LANES] = c_re.astype(bf16)
                third[g, at, LANES:] = c_im.astype(bf16)
                third[g, at_imag, :LANES] = c_im.astype(bf16)
                third[g, at_imag, LANES:] = (-c_re).astype(bf16)
                return carry

            lax.fori_loop(0, groups, group, 0, unroll=4)

    def gram(g):
        return lax.dot_general(
            prod[g], third[g], (((1,), (1,)), ((), ())), preferred_element_type=f32
        )

    sub = iota((GROUP, LANES), 0)
    keep = sub == lax.rem(iota((GROUP, LANES), 1), GROUP)
    low = lax.rem(iota((NB, LANES), 1), GROUP) < GROUP // 2

    def diagonal(total, side):
        octets = []
        for o in range(NB // GROUP):
            rows = []
            for b in range(GROUP):
                at = (o * GROUP + b) * GROUP
                rows.append(
                    jnp.where(
                        keep,
                        total[at : at + GROUP, side * LANES : (side + 1) * LANES],
                        0.0,
                    )
                )
            for k in (1, 2, 4):
                even = (sub & k) == 0
                rows = [
                    jnp.where(even, rows[i], rows[i + 1])
                    + pltpu.roll(jnp.where(even, rows[i + 1], rows[i]), k, 0)
                    for i in range(0, len(rows), 2)
                ]
            octets.append(rows[0])
        return jnp.concatenate(octets, axis=0)

    def across(off):
        peer = lax.rem(col + off, ns)
        return pltpu.make_async_remote_copy(
            src_ref=tiles.at[peer],
            dst_ref=part.at[off - 1],
            send_sem=send1.at[off - 1],
            recv_sem=recv1.at[off - 1],
            device_id=(me, peer),
            device_id_type=MESH,
        )

    for c in range(comps):
        look_up(c, me, stage)

        def arrive(off, carry, c=c):
            exchange(c, off).wait_recv()
            look_up(c, lax.rem(me - off + n, n), recv)
            return carry

        lax.fori_loop(1, n, arrive, 0)
        if c < comps - 1:

            def grams(g, carry, c=c):
                if c == 0:
                    acc[g] = gram(g)
                else:
                    acc[g] += gram(g)
                return carry

            lax.fori_loop(0, groups, grams, 0, unroll=2)

    def finish(h):
        def owner(i, carry):
            g = i * halves + h
            total = acc[g] + gram(g)
            real, imag = diagonal(total, 0), diagonal(total, 1)
            tiles[2 * h, i] = jnp.where(low, real, pltpu.roll(imag, GROUP // 2, 1))
            tiles[2 * h + 1, i] = jnp.where(
                low, pltpu.roll(real, LANES - GROUP // 2, 1), imag
            )
            return carry

        lax.fori_loop(0, owners, owner, 0, unroll=2)

    here = col // 2
    finish(1 - here)
    for off in range(1, ns):

        @pl.when(lax.rem(col + off, ns) // 2 != here)
        def _(off=off):
            across(off).start()

    finish(here)
    for off in range(1, ns):

        @pl.when(lax.rem(col + off, ns) // 2 == here)
        def _(off=off):
            across(off).start()

    for off in range(1, ns):
        across(off).wait_recv()
    whole = tiles[col]
    for off in range(1, ns):
        whole = whole + part[off - 1]
    summed[...] = whole

    def along(off):
        peer = lax.rem(me + off, n)
        return pltpu.make_async_remote_copy(
            src_ref=summed.at[peer],
            dst_ref=last.at[off],
            send_sem=send2.at[off],
            recv_sem=recv2.at[off],
            device_id=(peer, col),
            device_id_type=MESH,
        )

    def begin2(off, carry):
        along(off).start()
        return carry

    lax.fori_loop(1, n, begin2, 0)

    def add2(off, total):
        along(off).wait_recv()
        return total + last[off]

    out[...] = lax.fori_loop(1, n, add2, summed[me])

    for off in range(1, ns):
        across(off).wait_send()

    def drain(off, carry):
        for c in range(comps):
            exchange(c, off).wait_send()
        along(off).wait_send()
        return carry

    lax.fori_loop(1, n, drain, 0)


def lean_tile(n, ns, bins, weight_scale, snap, table, weights, triads, slots):
    comps, times, cells = snap.shape
    owners, per_owner = slots.shape
    groups = owners * per_owner // GROUP
    rows = times // NT * 2 * bins
    vmem = pl.BlockSpec(memory_space=pltpu.VMEM)
    anywhere = pl.BlockSpec(memory_space=pl.ANY)
    sem = pltpu.SemaphoreType.DMA
    return pl.pallas_call(
        functools.partial(lean_kernel, n, ns, bins, weight_scale),
        out_shape=jax.ShapeDtypeStruct((NB, LANES), jnp.float32),
        in_specs=[anywhere, anywhere, vmem, vmem, vmem],
        out_specs=vmem,
        scratch_shapes=[
            pltpu.VMEM((comps, times, cells), jnp.bfloat16),
            pltpu.VMEM((2, K, NT), jnp.bfloat16),
            pltpu.VMEM((2 * bins, NT), jnp.bfloat16),
            pltpu.VMEM((3 * owners * per_owner, bins), jnp.bfloat16),
            pltpu.VMEM((comps, n, rows, LANES), jnp.bfloat16),
            pltpu.VMEM((comps, n, rows, LANES), jnp.bfloat16),
            pltpu.VMEM((3 * owners * per_owner, 4 * LANES), jnp.float32),
            pltpu.VMEM((groups, NB * GROUP, 2 * LANES), jnp.bfloat16),
            pltpu.VMEM((groups, 2 * NB * GROUP, 2 * LANES), jnp.bfloat16),
            pltpu.VMEM((groups, NB * GROUP, 2 * LANES), jnp.float32),
            pltpu.VMEM((ns, n, NB, LANES), jnp.float32),
            pltpu.VMEM((ns - 1, n, NB, LANES), jnp.float32),
            pltpu.VMEM((n, NB, LANES), jnp.float32),
            pltpu.VMEM((n, NB, LANES), jnp.float32),
            sem((comps + 1,)),
            sem((comps, n)),
            sem((comps, n)),
            sem((ns - 1,)),
            sem((ns - 1,)),
            sem((n,)),
            sem((n,)),
        ],
        compiler_params=pltpu.CompilerParams(
            collective_id=bins, has_side_effects=True, vmem_limit_bytes=60 * 1024 * 1024
        ),
    )(snap, table, weights, triads, slots)


def lean(n, ns, snapshots, cell_weights, triads, owner_slots):
    times, comps, cells = snapshots.shape
    tile = lean_tile(
        n,
        ns,
        K,
        1.0 / math.sqrt(comps * cells * ns),
        snapshots.transpose(1, 0, 2),
        jnp.asarray(spectral_table().reshape(K, 2, NT).transpose(1, 0, 2)),
        cell_weights.reshape(n, LANES),
        triads.T,
        owner_slots,
    )
    mine = owner_slots.shape[1] // ns
    return tile.reshape(NB, NB, 2, mine).transpose(3, 2, 0, 1).reshape(mine, 2 * NB * NB)


def shards(n, ns, snapshots, cell_weights, triads, owner_slots):
    times, comps, cells = snapshots.shape
    owners, slot_count = owner_slots.shape
    if times % (2 * NT) == 0 and ns == 4 and slot_count == 2 * GROUP and owners == n:
        return lean(n, ns, snapshots, cell_weights, triads, owner_slots)
    weight_scale = 1.0 / math.sqrt(comps * cells * ns)
    vmem = pl.BlockSpec(memory_space=pltpu.VMEM)
    smem = pl.BlockSpec(memory_space=pltpu.SMEM)
    anywhere = pl.BlockSpec(memory_space=pl.ANY)
    sem = pltpu.SemaphoreType.DMA
    tile = pl.pallas_call(
        functools.partial(kernel, n, ns, weight_scale),
        out_shape=jax.ShapeDtypeStruct((NB, LANES), jnp.float32),
        in_specs=[anywhere, vmem, vmem, smem],
        out_specs=vmem,
        scratch_shapes=[
            pltpu.VMEM((comps, NB * NT, LANES), jnp.bfloat16),
            pltpu.VMEM((2 * K * NB, LANES), jnp.float32),
            pltpu.VMEM((K, 2 * NB, LANES), jnp.float32),
            pltpu.VMEM((K, 2 * NB, LANES), jnp.bfloat16),
            pltpu.VMEM((ns, n, NB, LANES), jnp.float32),
            pltpu.VMEM((ns - 1, n, NB, LANES), jnp.float32),
            pltpu.VMEM((n, NB, LANES), jnp.float32),
            pltpu.VMEM((n, NB, LANES), jnp.float32),
            sem((comps, n)),
            sem((comps, n)),
            sem((comps,)),
            sem((ns - 1,)),
            sem((ns - 1,)),
            sem((n,)),
            sem((n,)),
        ],
        compiler_params=pltpu.CompilerParams(
            collective_id=0, has_side_effects=True, vmem_limit_bytes=40 * 1024 * 1024
        ),
    )(
        snapshots.transpose(1, 0, 2),
        jnp.asarray(spectral_table()),
        cell_weights.reshape(n, LANES),
        jnp.take(triads.T, jnp.maximum(owner_slots, 0).reshape(-1), axis=1, mode="clip"),
    )
    mine = slot_count // ns
    flat = tile.reshape(NB, 2, mine, NB).transpose(2, 1, 0, 3).reshape(mine, 2 * NB * NB)
    my_slots = lax.dynamic_slice(
        owner_slots, (lax.axis_index("tm"), lax.axis_index("space") * mine), (1, mine)
    ).reshape(mine, 1)
    return jnp.where(my_slots >= 0, flat, 0.0)


def solution(mesh):
    placed = (P("tm", None, "space"), P("space"), P(), P())
    n, ns = mesh.shape["tm"], mesh.shape["space"]
    return jax.shard_map(
        functools.partial(shards, n, ns),
        mesh=mesh,
        in_specs=placed,
        out_specs=P(("tm", "space"), None),
        check_vma=False,
    )
```

```python
import functools
import math

import jax
import jax.numpy as jnp
import ml_dtypes
import numpy as np
from jax import lax
from jax.experimental import pallas as pl
from jax.experimental.pallas import tpu as pltpu
from jax.sharding import PartitionSpec as P

NB = 16
NT = 256
K = 128
GROUP = 8
LANES = 128
BINS = (88, 96, 104, 112, K)
MESH = pl.DeviceIdType.MESH


def spectral_table():
    sample = np.arange(NT)
    freq_bins = np.arange(K)
    angles = 2.0 * math.pi / NT * (freq_bins[:, None] * sample[None, :] % NT)
    window = 0.5 - 0.5 * np.cos(2.0 * math.pi / NT * sample)
    scale = math.sqrt(8.0 / (3.0 * NT))
    rows = np.stack(
        [scale * window * np.cos(angles), -scale * window * np.sin(angles)], axis=1
    )
    return rows.reshape(2 * K, NT).astype(np.float32).astype(ml_dtypes.bfloat16)


def kernel(
    n,
    ns,
    weight_scale,
    snap,
    table,
    weights,
    freqs,
    out,
    recv,
    rows,
    spec,
    narrow,
    acc,
    part,
    summed,
    last,
    send_sem,
    recv_sem,
    own_sem,
    send1,
    recv1,
    send2,
    recv2,
):
    comps, times = snap.shape[0], snap.shape[1]
    me = lax.axis_index("tm")
    col = lax.axis_index("space")

    barrier = pltpu.get_barrier_semaphore()

    def greet_tm(off, carry):
        pl.semaphore_signal(
            barrier, inc=1, device_id=(lax.rem(me + off, n), col), device_id_type=MESH
        )
        return carry

    lax.fori_loop(1, n, greet_tm, 0)
    for off in range(1, ns):
        pl.semaphore_signal(
            barrier, inc=1, device_id=(me, lax.rem(col + off, ns)), device_id_type=MESH
        )
    pl.semaphore_wait(barrier, n - 1 + ns - 1)

    def exchange(c, off):
        peer = lax.rem(me + off, n)
        return pltpu.make_async_remote_copy(
            src_ref=snap.at[c, :, pl.ds(pl.multiple_of(peer * LANES, LANES), LANES)],
            dst_ref=recv.at[c, pl.ds(pl.multiple_of(me * times, 16), times), :],
            send_sem=send_sem.at[c, off],
            recv_sem=recv_sem.at[c, off],
            device_id=(peer, col),
            device_id_type=MESH,
        )

    def own(c):
        return pltpu.make_async_copy(
            snap.at[c, :, pl.ds(pl.multiple_of(me * LANES, LANES), LANES)],
            recv.at[c, pl.ds(pl.multiple_of(me * times, 16), times), :],
            own_sem.at[c],
        )

    for c in range(comps):

        def begin(off, carry, c=c):
            exchange(c, off).start()
            return carry

        lax.fori_loop(1, n, begin, 0)
        own(c).start()

    w_row = weights[pl.ds(me, 1), :] * weight_scale
    lane = lax.broadcasted_iota(jnp.int32, (2 * NB, 2 * LANES), 1)
    lane_group = lax.rem(lane, LANES) // NB
    low = lax.broadcasted_iota(jnp.int32, (NB, LANES), 1) < LANES // 2
    groups = freqs.shape[1] // GROUP
    per_owner = groups // n

    def dft(c, b):
        x = recv[c, pl.ds(pl.multiple_of(b * NT, NT), NT), :]
        y = jnp.dot(table[...], x, preferred_element_type=jnp.float32)
        rows[pl.ds(b, 2 * K, stride=NB), :] = y

    def regroup(k, carry):
        both = rows[pl.ds(pl.multiple_of(k * 2 * NB, 2 * NB), 2 * NB), :].astype(jnp.bfloat16)
        narrow[k] = both
        spec[k] = both.astype(jnp.float32)
        return carry

    def gram_group(c, g):
        owner = g // per_owner
        half = lax.rem(g, per_owner)
        prods, c_re, c_im = [], [], []
        for s in range(GROUP):
            place = g * GROUP + s
            a = spec[freqs[0, place]]
            b2 = spec[freqs[1, place]]
            c2 = narrow[freqs[2, place]]
            re = (a[:NB] * b2[:NB] - a[NB:] * b2[NB:]) * w_row
            im = (a[:NB] * b2[NB:] + a[NB:] * b2[:NB]) * w_row
            prods += [re.astype(jnp.bfloat16), im.astype(jnp.bfloat16)]
            c_re.append(c2[:NB])
            c_im.append(c2[NB:])
        left = jnp.concatenate(prods, axis=0)
        right = jnp.concatenate(c_re + c_im, axis=0)
        gram = lax.dot_general(
            left, right, (((1,), (1,)), ((), ())), preferred_element_type=jnp.float32
        )
        diag = gram[: 2 * NB]
        for s in range(1, GROUP):
            diag = jnp.where(lane_group == s, gram[2 * NB * s : 2 * NB * (s + 1)], diag)
        real = diag[:NB, :LANES] + diag[NB:, LANES:]
        imag = diag[:NB, LANES:] - diag[NB:, :LANES]
        half_turn = LANES // 2
        first = jnp.where(low, real, pltpu.roll(imag, half_turn, 1))
        second = jnp.where(low, pltpu.roll(real, half_turn, 1), imag)
        if c == 0:
            acc[2 * half, owner] = first
            acc[2 * half + 1, owner] = second
        else:
            acc[2 * half, owner] += first
            acc[2 * half + 1, owner] += second

    for c in range(comps):
        own(c).wait()
        if times % NT == 0:

            def transform(i, carry, c=c):
                dft(c, me * (times // NT) + i)
                return carry

            lax.fori_loop(0, times // NT, transform, 0)

            def arrive(off, carry, c=c):
                exchange(c, off).wait_recv()
                src = lax.rem(me - off + n, n)
                for i in range(times // NT):
                    dft(c, src * (times // NT) + i)
                return carry

            lax.fori_loop(1, n, arrive, 0)
        else:

            def arrive(off, carry, c=c):
                exchange(c, off).wait_recv()
                return carry

            lax.fori_loop(1, n, arrive, 0)

            def transform(b, carry, c=c):
                dft(c, b)
                return carry

            lax.fori_loop(0, NB, transform, 0)

        lax.fori_loop(0, K, regroup, 0, unroll=4)

        def grams(g, carry, c=c):
            gram_group(c, g)
            return carry

        lax.fori_loop(0, groups, grams, 0)

    def across(off):
        peer = lax.rem(col + off, ns)
        return pltpu.make_async_remote_copy(
            src_ref=acc.at[peer],
            dst_ref=part.at[off - 1],
            send_sem=send1.at[off - 1],
            recv_sem=recv1.at[off - 1],
            device_id=(me, peer),
            device_id_type=MESH,
        )

    for off in range(1, ns):
        across(off).start()
    for off in range(1, ns):
        across(off).wait_recv()
    total = acc[col]
    for off in range(1, ns):
        total = total + part[off - 1]
    summed[...] = total

    def along(off):
        peer = lax.rem(me + off, n)
        return pltpu.make_async_remote_copy(
            src_ref=summed.at[peer],
            dst_ref=last.at[off],
            send_sem=send2.at[off],
            recv_sem=recv2.at[off],
            device_id=(peer, col),
            device_id_type=MESH,
        )

    def begin2(off, carry):
        along(off).start()
        return carry

    lax.fori_loop(1, n, begin2, 0)

    def add2(off, total):
        along(off).wait_recv()
        return total + last[off]

    out[...] = lax.fori_loop(1, n, add2, summed[me])

    for off in range(1, ns):
        across(off).wait_send()

    def drain(off, carry):
        for c in range(comps):
            exchange(c, off).wait_send()
        along(off).wait_send()
        return carry

    lax.fori_loop(1, n, drain, 0)


def lean_kernel(
    n,
    ns,
    bins,
    weight_scale,
    snap,
    table,
    weights,
    triads,
    slots,
    out,
    series,
    tab,
    dft,
    pick,
    stage,
    recv,
    looked,
    prod,
    third,
    acc,
    tiles,
    part,
    summed,
    last,
    load_sem,
    send_sem,
    recv_sem,
    send1,
    recv1,
    send2,
    recv2,
):
    comps, times, cells = series.shape
    blocks = times // NT
    count = triads.shape[1]
    owners, per_owner = slots.shape
    total_slots = owners * per_owner
    groups = total_slots // GROUP
    halves = per_owner // GROUP
    me = lax.axis_index("tm")
    col = lax.axis_index("space")
    f32, bf16 = jnp.float32, jnp.bfloat16

    def iota(shape, axis):
        return lax.broadcasted_iota(jnp.int32, shape, axis)

    fetch_table = pltpu.make_async_copy(table, tab, load_sem.at[comps])
    fetch_table.start()

    def fetch(c):
        return pltpu.make_async_copy(snap.at[c], series.at[c], load_sem.at[c])

    for c in range(comps):
        fetch(c).start()

    barrier = pltpu.get_barrier_semaphore()

    def greet(off, carry):
        pl.semaphore_signal(
            barrier, inc=1, device_id=(lax.rem(me + off, n), col), device_id_type=MESH
        )
        return carry

    lax.fori_loop(1, n, greet, 0)
    for off in range(1, ns):
        pl.semaphore_signal(
            barrier, inc=1, device_id=(me, lax.rem(col + off, ns)), device_id_type=MESH
        )

    freq = iota((K, count), 0)
    hit = (
        (freq == triads[0:1, :]) | (freq == triads[1:2, :]) | (freq == triads[2:3, :])
    )
    used = jnp.max(jnp.where(hit, 1.0, 0.0), axis=1, keepdims=True)
    used = jnp.broadcast_to(used, (K, K))
    column = iota((K, K), 1)
    below = jnp.where(column < iota((K, K), 0), 1.0, 0.0)
    rank = jnp.dot(below.astype(bf16), used.astype(bf16), preferred_element_type=f32)
    place = jnp.where((rank == column.astype(f32)) & (used > 0.0), 1.0, 0.0)
    chosen = place.T[:bins].astype(bf16)
    fetch_table.wait()
    dft[...] = jnp.concatenate(
        [jnp.dot(chosen, tab[r], preferred_element_type=f32) for r in range(2)], axis=0
    ).astype(bf16)

    def transform(c):
        fetch(c).wait()

        def step(p, carry):
            for b in range(blocks):
                y = jnp.dot(
                    dft[...],
                    series[
                        c,
                        b * NT : (b + 1) * NT,
                        pl.ds(pl.multiple_of(p * 2 * LANES, 2 * LANES), 2 * LANES),
                    ],
                    preferred_element_type=f32,
                ).astype(bf16)
                rows = pl.ds(b * 2 * bins, 2 * bins)
                stage[c, 2 * p, rows, :] = y[:, :LANES]
                stage[c, 2 * p + 1, rows, :] = y[:, LANES:]
            return carry

        lax.fori_loop(0, n // 2, step, 0)

    def exchange(c, off):
        peer = lax.rem(me + off, n)
        return pltpu.make_async_remote_copy(
            src_ref=stage.at[c, peer],
            dst_ref=recv.at[c, me],
            send_sem=send_sem.at[c, off],
            recv_sem=recv_sem.at[c, off],
            device_id=(peer, col),
            device_id_type=MESH,
        )

    transform(0)
    pl.semaphore_wait(barrier, n - 1 + ns - 1)
    for c in range(comps):
        if c > 0:
            transform(c)

        def begin(off, carry, c=c):
            exchange(c, off).start()
            return carry

        lax.fori_loop(1, n, begin, 0)

    wide = (owners, total_slots)
    spread = jnp.where(
        lax.rem(iota((per_owner, total_slots), 1), per_owner)
        == iota((per_owner, total_slots), 0),
        1.0,
        0.0,
    )
    tiled = jnp.dot(
        slots[...].astype(f32).astype(bf16),
        spread.astype(bf16),
        preferred_element_type=f32,
    )
    own_row = iota(wide, 1) // per_owner == iota(wide, 0)
    slot_triad = jnp.sum(jnp.where(own_row, tiled, 0.0), axis=0, keepdims=True)
    holds = jnp.where(
        iota((count, total_slots), 0).astype(f32) == slot_triad, 1.0, 0.0
    ).astype(bf16)
    slot_freq = jnp.dot(
        (triads[...] + 1).astype(f32).astype(bf16), holds, preferred_element_type=f32
    )
    for role in range(3):
        named = jnp.where(
            iota((K, total_slots), 0).astype(f32) + 1.0 == slot_freq[role : role + 1, :],
            1.0,
            0.0,
        )
        chosen_all = jnp.dot(
            place.T.astype(bf16), named.astype(bf16), preferred_element_type=f32
        )
        pick[role * total_slots : (role + 1) * total_slots, :] = chosen_all.T[
            :, :bins
        ].astype(bf16)

    w_row = weights[pl.ds(me, 1), :] * weight_scale

    def look_up(c, src, ref):
        for pair in range(blocks // 2):
            sides = []
            for b in (2 * pair, 2 * pair + 1):
                both = ref[c, src, b * 2 * bins : (b + 1) * 2 * bins, :]
                if bins % 16 != 0:
                    both = both.astype(f32)
                sides += [both[:bins], both[bins:]]
            looked[...] = jnp.dot(
                pick[...],
                jnp.concatenate(sides, axis=1).astype(bf16),
                preferred_element_type=f32,
            )
            first = src * (blocks * GROUP) + pair * 2 * GROUP
            at = pl.ds(pl.multiple_of(first, 2 * GROUP), 2 * GROUP)
            at_imag = pl.ds(pl.multiple_of(NB * GROUP + first, 2 * GROUP), 2 * GROUP)

            def group(g, carry):
                def tile(role, q):
                    row = pl.multiple_of(role * total_slots + g * GROUP, GROUP)
                    return looked[pl.ds(row, GROUP), q * LANES : (q + 1) * LANES]

                re, im, c_re, c_im = [], [], [], []
                for b in range(2):
                    ar, ai = tile(0, 2 * b), tile(0, 2 * b + 1)
                    br, bi = tile(1, 2 * b), tile(1, 2 * b + 1)
                    re.append((ar * br - ai * bi) * w_row)
                    im.append((ar * bi + ai * br) * w_row)
                    c_re.append(tile(2, 2 * b))
                    c_im.append(tile(2, 2 * b + 1))
                re, im, c_re, c_im = (
                    jnp.concatenate(v, axis=0) for v in (re, im, c_re, c_im)
                )
                prod[g, at, :LANES] = re.astype(bf16)
                prod[g, at, LANES:] = im.astype(bf16)
                third[g, at, :LANES] = c_re.astype(bf16)
                third[g, at, LANES:] = c_im.astype(bf16)
                third[g, at_imag, :LANES] = c_im.astype(bf16)
                third[g, at_imag, LANES:] = (-c_re).astype(bf16)
                return carry

            lax.fori_loop(0, groups, group, 0, unroll=4)

    def gram(g):
        return lax.dot_general(
            prod[g], third[g], (((1,), (1,)), ((), ())), preferred_element_type=f32
        )

    sub = iota((GROUP, LANES), 0)
    keep = sub == lax.rem(iota((GROUP, LANES), 1), GROUP)
    low = lax.rem(iota((NB, LANES), 1), GROUP) < GROUP // 2

    def diagonal(total, side):
        octets = []
        for o in range(NB // GROUP):
            rows = []
            for b in range(GROUP):
                at = (o * GROUP + b) * GROUP
                rows.append(
                    jnp.where(
                        keep,
                        total[at : at + GROUP, side * LANES : (side + 1) * LANES],
                        0.0,
                    )
                )
            for k in (1, 2, 4):
                even = (sub & k) == 0
                rows = [
                    jnp.where(even, rows[i], rows[i + 1])
                    + pltpu.roll(jnp.where(even, rows[i + 1], rows[i]), k, 0)
                    for i in range(0, len(rows), 2)
                ]
            octets.append(rows[0])
        return jnp.concatenate(octets, axis=0)

    def across(off):
        peer = lax.rem(col + off, ns)
        return pltpu.make_async_remote_copy(
            src_ref=tiles.at[peer],
            dst_ref=part.at[off - 1],
            send_sem=send1.at[off - 1],
            recv_sem=recv1.at[off - 1],
            device_id=(me, peer),
            device_id_type=MESH,
        )

    for c in range(comps):
        look_up(c, me, stage)

        def arrive(off, carry, c=c):
            exchange(c, off).wait_recv()
            look_up(c, lax.rem(me - off + n, n), recv)
            return carry

        lax.fori_loop(1, n, arrive, 0)
        if c < comps - 1:

            def grams(g, carry, c=c):
                if c == 0:
                    acc[g] = gram(g)
                else:
                    acc[g] += gram(g)
                return carry

            lax.fori_loop(0, groups, grams, 0, unroll=2)

    def finish(h):
        def owner(i, carry):
            g = i * halves + h
            total = acc[g] + gram(g)
            real, imag = diagonal(total, 0), diagonal(total, 1)
            tiles[2 * h, i] = jnp.where(low, real, pltpu.roll(imag, GROUP // 2, 1))
            tiles[2 * h + 1, i] = jnp.where(
                low, pltpu.roll(real, LANES - GROUP // 2, 1), imag
            )
            return carry

        lax.fori_loop(0, owners, owner, 0, unroll=2)

    here = col // 2
    finish(1 - here)
    for off in range(1, ns):

        @pl.when(lax.rem(col + off, ns) // 2 != here)
        def _(off=off):
            across(off).start()

    finish(here)
    for off in range(1, ns):

        @pl.when(lax.rem(col + off, ns) // 2 == here)
        def _(off=off):
            across(off).start()

    for off in range(1, ns):
        across(off).wait_recv()
    whole = tiles[col]
    for off in range(1, ns):
        whole = whole + part[off - 1]
    summed[...] = whole

    def along(off):
        peer = lax.rem(me + off, n)
        return pltpu.make_async_remote_copy(
            src_ref=summed.at[peer],
            dst_ref=last.at[off],
            send_sem=send2.at[off],
            recv_sem=recv2.at[off],
            device_id=(peer, col),
            device_id_type=MESH,
        )

    def begin2(off, carry):
        along(off).start()
        return carry

    lax.fori_loop(1, n, begin2, 0)

    def add2(off, total):
        along(off).wait_recv()
        return total + last[off]

    out[...] = lax.fori_loop(1, n, add2, summed[me])

    for off in range(1, ns):
        across(off).wait_send()

    def drain(off, carry):
        for c in range(comps):
            exchange(c, off).wait_send()
        along(off).wait_send()
        return carry

    lax.fori_loop(1, n, drain, 0)


def lean_tile(n, ns, bins, weight_scale, snap, table, weights, triads, slots):
    comps, times, cells = snap.shape
    owners, per_owner = slots.shape
    groups = owners * per_owner // GROUP
    rows = times // NT * 2 * bins
    vmem = pl.BlockSpec(memory_space=pltpu.VMEM)
    anywhere = pl.BlockSpec(memory_space=pl.ANY)
    sem = pltpu.SemaphoreType.DMA
    return pl.pallas_call(
        functools.partial(lean_kernel, n, ns, bins, weight_scale),
        out_shape=jax.ShapeDtypeStruct((NB, LANES), jnp.float32),
        in_specs=[anywhere, anywhere, vmem, vmem, vmem],
        out_specs=vmem,
        scratch_shapes=[
            pltpu.VMEM((comps, times, cells), jnp.bfloat16),
            pltpu.VMEM((2, K, NT), jnp.bfloat16),
            pltpu.VMEM((2 * bins, NT), jnp.bfloat16),
            pltpu.VMEM((3 * owners * per_owner, bins), jnp.bfloat16),
            pltpu.VMEM((comps, n, rows, LANES), jnp.bfloat16),
            pltpu.VMEM((comps, n, rows, LANES), jnp.bfloat16),
            pltpu.VMEM((3 * owners * per_owner, 4 * LANES), jnp.float32),
            pltpu.VMEM((groups, NB * GROUP, 2 * LANES), jnp.bfloat16),
            pltpu.VMEM((groups, 2 * NB * GROUP, 2 * LANES), jnp.bfloat16),
            pltpu.VMEM((groups, NB * GROUP, 2 * LANES), jnp.float32),
            pltpu.VMEM((ns, n, NB, LANES), jnp.float32),
            pltpu.VMEM((ns - 1, n, NB, LANES), jnp.float32),
            pltpu.VMEM((n, NB, LANES), jnp.float32),
            pltpu.VMEM((n, NB, LANES), jnp.float32),
            sem((comps + 1,)),
            sem((comps, n)),
            sem((comps, n)),
            sem((ns - 1,)),
            sem((ns - 1,)),
            sem((n,)),
            sem((n,)),
        ],
        compiler_params=pltpu.CompilerParams(
            collective_id=bins, has_side_effects=True, vmem_limit_bytes=60 * 1024 * 1024
        ),
    )(snap, table, weights, triads, slots)


def size_class(bins, triads, out):
    count = triads.shape[1]
    freq = lax.broadcasted_iota(jnp.int32, (K, count), 0)
    hit = (
        (freq == triads[0:1, :]) | (freq == triads[1:2, :]) | (freq == triads[2:3, :])
    )
    used = jnp.sum(jnp.max(jnp.where(hit, 1.0, 0.0), axis=1, keepdims=True))
    index = jnp.int32(0)
    for size in bins[:-1]:
        index += (used > size).astype(jnp.int32)
    out[0] = index


def lean(n, ns, snapshots, cell_weights, triads, owner_slots):
    times, comps, cells = snapshots.shape
    index = pl.pallas_call(
        functools.partial(size_class, BINS),
        out_shape=jax.ShapeDtypeStruct((1,), jnp.int32),
        in_specs=[pl.BlockSpec(memory_space=pltpu.VMEM)],
        out_specs=pl.BlockSpec(memory_space=pltpu.SMEM),
    )(triads.T)
    scale = 1.0 / math.sqrt(comps * cells * ns)
    tile = lax.switch(
        index[0],
        [functools.partial(lean_tile, n, ns, bins, scale) for bins in BINS],
        snapshots.transpose(1, 0, 2),
        jnp.asarray(spectral_table().reshape(K, 2, NT).transpose(1, 0, 2)),
        cell_weights.reshape(n, LANES),
        triads.T,
        owner_slots,
    )
    mine = owner_slots.shape[1] // ns
    return tile.reshape(NB, NB, 2, mine).transpose(3, 2, 0, 1).reshape(mine, 2 * NB * NB)


def shards(n, ns, snapshots, cell_weights, triads, owner_slots):
    times, comps, cells = snapshots.shape
    owners, slot_count = owner_slots.shape
    if times % (2 * NT) == 0 and ns == 4 and slot_count == 2 * GROUP and owners == n:
        return lean(n, ns, snapshots, cell_weights, triads, owner_slots)
    weight_scale = 1.0 / math.sqrt(comps * cells * ns)
    vmem = pl.BlockSpec(memory_space=pltpu.VMEM)
    smem = pl.BlockSpec(memory_space=pltpu.SMEM)
    anywhere = pl.BlockSpec(memory_space=pl.ANY)
    sem = pltpu.SemaphoreType.DMA
    tile = pl.pallas_call(
        functools.partial(kernel, n, ns, weight_scale),
        out_shape=jax.ShapeDtypeStruct((NB, LANES), jnp.float32),
        in_specs=[anywhere, vmem, vmem, smem],
        out_specs=vmem,
        scratch_shapes=[
            pltpu.VMEM((comps, NB * NT, LANES), jnp.bfloat16),
            pltpu.VMEM((2 * K * NB, LANES), jnp.float32),
            pltpu.VMEM((K, 2 * NB, LANES), jnp.float32),
            pltpu.VMEM((K, 2 * NB, LANES), jnp.bfloat16),
            pltpu.VMEM((ns, n, NB, LANES), jnp.float32),
            pltpu.VMEM((ns - 1, n, NB, LANES), jnp.float32),
            pltpu.VMEM((n, NB, LANES), jnp.float32),
            pltpu.VMEM((n, NB, LANES), jnp.float32),
            sem((comps, n)),
            sem((comps, n)),
            sem((comps,)),
            sem((ns - 1,)),
            sem((ns - 1,)),
            sem((n,)),
            sem((n,)),
        ],
        compiler_params=pltpu.CompilerParams(
            collective_id=0, has_side_effects=True, vmem_limit_bytes=40 * 1024 * 1024
        ),
    )(
        snapshots.transpose(1, 0, 2),
        jnp.asarray(spectral_table()),
        cell_weights.reshape(n, LANES),
        jnp.take(triads.T, jnp.maximum(owner_slots, 0).reshape(-1), axis=1, mode="clip"),
    )
    mine = slot_count // ns
    flat = tile.reshape(NB, 2, mine, NB).transpose(2, 1, 0, 3).reshape(mine, 2 * NB * NB)
    my_slots = lax.dynamic_slice(
        owner_slots, (lax.axis_index("tm"), lax.axis_index("space") * mine), (1, mine)
    ).reshape(mine, 1)
    return jnp.where(my_slots >= 0, flat, 0.0)


def solution(mesh):
    placed = (P("tm", None, "space"), P("space"), P(), P())
    n, ns = mesh.shape["tm"], mesh.shape["space"]
    return jax.shard_map(
        functools.partial(shards, n, ns),
        mesh=mesh,
        in_specs=placed,
        out_specs=P(("tm", "space"), None),
        check_vma=False,
    )
```

```python
import functools
import math

import jax
import jax.numpy as jnp
import ml_dtypes
import numpy as np
from jax import lax
from jax.experimental import pallas as pl
from jax.experimental.pallas import tpu as pltpu
from jax.sharding import PartitionSpec as P

NB = 16
NT = 256
K = 128
GROUP = 8
LANES = 128
BINS = (92, 96, 100, 104, 112, K)
MESH = pl.DeviceIdType.MESH


def spectral_table():
    sample = np.arange(NT)
    freq_bins = np.arange(K)
    angles = 2.0 * math.pi / NT * (freq_bins[:, None] * sample[None, :] % NT)
    window = 0.5 - 0.5 * np.cos(2.0 * math.pi / NT * sample)
    scale = math.sqrt(8.0 / (3.0 * NT))
    rows = np.stack(
        [scale * window * np.cos(angles), -scale * window * np.sin(angles)], axis=1
    )
    return rows.reshape(2 * K, NT).astype(np.float32).astype(ml_dtypes.bfloat16)


def kernel(
    n,
    ns,
    weight_scale,
    snap,
    table,
    weights,
    freqs,
    out,
    recv,
    rows,
    spec,
    narrow,
    acc,
    part,
    summed,
    last,
    send_sem,
    recv_sem,
    own_sem,
    send1,
    recv1,
    send2,
    recv2,
):
    comps, times = snap.shape[0], snap.shape[1]
    me = lax.axis_index("tm")
    col = lax.axis_index("space")

    barrier = pltpu.get_barrier_semaphore()

    def greet_tm(off, carry):
        pl.semaphore_signal(
            barrier, inc=1, device_id=(lax.rem(me + off, n), col), device_id_type=MESH
        )
        return carry

    lax.fori_loop(1, n, greet_tm, 0)
    for off in range(1, ns):
        pl.semaphore_signal(
            barrier, inc=1, device_id=(me, lax.rem(col + off, ns)), device_id_type=MESH
        )
    pl.semaphore_wait(barrier, n - 1 + ns - 1)

    def exchange(c, off):
        peer = lax.rem(me + off, n)
        return pltpu.make_async_remote_copy(
            src_ref=snap.at[c, :, pl.ds(pl.multiple_of(peer * LANES, LANES), LANES)],
            dst_ref=recv.at[c, pl.ds(pl.multiple_of(me * times, 16), times), :],
            send_sem=send_sem.at[c, off],
            recv_sem=recv_sem.at[c, off],
            device_id=(peer, col),
            device_id_type=MESH,
        )

    def own(c):
        return pltpu.make_async_copy(
            snap.at[c, :, pl.ds(pl.multiple_of(me * LANES, LANES), LANES)],
            recv.at[c, pl.ds(pl.multiple_of(me * times, 16), times), :],
            own_sem.at[c],
        )

    for c in range(comps):

        def begin(off, carry, c=c):
            exchange(c, off).start()
            return carry

        lax.fori_loop(1, n, begin, 0)
        own(c).start()

    w_row = weights[pl.ds(me, 1), :] * weight_scale
    lane = lax.broadcasted_iota(jnp.int32, (2 * NB, 2 * LANES), 1)
    lane_group = lax.rem(lane, LANES) // NB
    low = lax.broadcasted_iota(jnp.int32, (NB, LANES), 1) < LANES // 2
    groups = freqs.shape[1] // GROUP
    per_owner = groups // n

    def dft(c, b):
        x = recv[c, pl.ds(pl.multiple_of(b * NT, NT), NT), :]
        y = jnp.dot(table[...], x, preferred_element_type=jnp.float32)
        rows[pl.ds(b, 2 * K, stride=NB), :] = y

    def regroup(k, carry):
        both = rows[pl.ds(pl.multiple_of(k * 2 * NB, 2 * NB), 2 * NB), :].astype(jnp.bfloat16)
        narrow[k] = both
        spec[k] = both.astype(jnp.float32)
        return carry

    def gram_group(c, g):
        owner = g // per_owner
        half = lax.rem(g, per_owner)
        prods, c_re, c_im = [], [], []
        for s in range(GROUP):
            place = g * GROUP + s
            a = spec[freqs[0, place]]
            b2 = spec[freqs[1, place]]
            c2 = narrow[freqs[2, place]]
            re = (a[:NB] * b2[:NB] - a[NB:] * b2[NB:]) * w_row
            im = (a[:NB] * b2[NB:] + a[NB:] * b2[:NB]) * w_row
            prods += [re.astype(jnp.bfloat16), im.astype(jnp.bfloat16)]
            c_re.append(c2[:NB])
            c_im.append(c2[NB:])
        left = jnp.concatenate(prods, axis=0)
        right = jnp.concatenate(c_re + c_im, axis=0)
        gram = lax.dot_general(
            left, right, (((1,), (1,)), ((), ())), preferred_element_type=jnp.float32
        )
        diag = gram[: 2 * NB]
        for s in range(1, GROUP):
            diag = jnp.where(lane_group == s, gram[2 * NB * s : 2 * NB * (s + 1)], diag)
        real = diag[:NB, :LANES] + diag[NB:, LANES:]
        imag = diag[:NB, LANES:] - diag[NB:, :LANES]
        half_turn = LANES // 2
        first = jnp.where(low, real, pltpu.roll(imag, half_turn, 1))
        second = jnp.where(low, pltpu.roll(real, half_turn, 1), imag)
        if c == 0:
            acc[2 * half, owner] = first
            acc[2 * half + 1, owner] = second
        else:
            acc[2 * half, owner] += first
            acc[2 * half + 1, owner] += second

    for c in range(comps):
        own(c).wait()
        if times % NT == 0:

            def transform(i, carry, c=c):
                dft(c, me * (times // NT) + i)
                return carry

            lax.fori_loop(0, times // NT, transform, 0)

            def arrive(off, carry, c=c):
                exchange(c, off).wait_recv()
                src = lax.rem(me - off + n, n)
                for i in range(times // NT):
                    dft(c, src * (times // NT) + i)
                return carry

            lax.fori_loop(1, n, arrive, 0)
        else:

            def arrive(off, carry, c=c):
                exchange(c, off).wait_recv()
                return carry

            lax.fori_loop(1, n, arrive, 0)

            def transform(b, carry, c=c):
                dft(c, b)
                return carry

            lax.fori_loop(0, NB, transform, 0)

        lax.fori_loop(0, K, regroup, 0, unroll=4)

        def grams(g, carry, c=c):
            gram_group(c, g)
            return carry

        lax.fori_loop(0, groups, grams, 0)

    def across(off):
        peer = lax.rem(col + off, ns)
        return pltpu.make_async_remote_copy(
            src_ref=acc.at[peer],
            dst_ref=part.at[off - 1],
            send_sem=send1.at[off - 1],
            recv_sem=recv1.at[off - 1],
            device_id=(me, peer),
            device_id_type=MESH,
        )

    for off in range(1, ns):
        across(off).start()
    for off in range(1, ns):
        across(off).wait_recv()
    total = acc[col]
    for off in range(1, ns):
        total = total + part[off - 1]
    summed[...] = total

    def along(off):
        peer = lax.rem(me + off, n)
        return pltpu.make_async_remote_copy(
            src_ref=summed.at[peer],
            dst_ref=last.at[off],
            send_sem=send2.at[off],
            recv_sem=recv2.at[off],
            device_id=(peer, col),
            device_id_type=MESH,
        )

    def begin2(off, carry):
        along(off).start()
        return carry

    lax.fori_loop(1, n, begin2, 0)

    def add2(off, total):
        along(off).wait_recv()
        return total + last[off]

    out[...] = lax.fori_loop(1, n, add2, summed[me])

    for off in range(1, ns):
        across(off).wait_send()

    def drain(off, carry):
        for c in range(comps):
            exchange(c, off).wait_send()
        along(off).wait_send()
        return carry

    lax.fori_loop(1, n, drain, 0)


def lean_kernel(
    n,
    ns,
    bins,
    weight_scale,
    snap,
    table,
    weights_at,
    triads_at,
    slots_at,
    out,
    series,
    tab,
    weights,
    triads,
    slots,
    dft,
    pick,
    stage,
    recv,
    looked,
    prod,
    third,
    acc,
    tiles,
    paired,
    sums,
    land,
    load_sem,
    send_sem,
    recv_sem,
    send_pair,
    recv_pair,
    send_tile,
    recv_tile,
):
    comps, times, cells = series.shape
    blocks = times // NT
    count = triads.shape[1]
    owners, per_owner = slots.shape
    total_slots = owners * per_owner
    groups = total_slots // GROUP
    halves = per_owner // GROUP
    me = lax.axis_index("tm")
    col = lax.axis_index("space")
    f32, bf16 = jnp.float32, jnp.bfloat16

    def iota(shape, axis):
        return lax.broadcasted_iota(jnp.int32, shape, axis)

    core, here = lax.rem(col, 2), col // 2
    sibling = (me, 2 * here + 1 - core)
    me_at = 2 * me + here

    def chip(off):
        other = lax.rem(me_at + off, 2 * n)
        return other // 2, lax.rem(other, 2)

    barrier = pltpu.get_barrier_semaphore()

    def greet(off, carry):
        i, h = chip(off)
        pl.semaphore_signal(
            barrier, inc=1, device_id=(i, 2 * h + core), device_id_type=MESH
        )
        return carry

    pl.semaphore_signal(barrier, inc=1, device_id=sibling, device_id_type=MESH)
    lax.fori_loop(1, 2 * n, greet, 0)

    small = [
        pltpu.make_async_copy(source, target, load_sem.at[comps + i])
        for i, (source, target) in enumerate(
            ((triads_at, triads), (table, tab), (slots_at, slots), (weights_at, weights))
        )
    ]

    def fetch(c):
        return pltpu.make_async_copy(snap.at[c], series.at[c], load_sem.at[c])

    for copy in small:
        copy.start()
    for c in range(comps):
        fetch(c).start()
    small[0].wait()

    freq = iota((K, count), 0)
    hit = (
        (freq == triads[0:1, :]) | (freq == triads[1:2, :]) | (freq == triads[2:3, :])
    )
    used = jnp.max(jnp.where(hit, 1.0, 0.0), axis=1, keepdims=True)
    used = jnp.broadcast_to(used, (K, K))
    column = iota((K, K), 1)
    below = jnp.where(column < iota((K, K), 0), 1.0, 0.0)
    rank = jnp.dot(below.astype(bf16), used.astype(bf16), preferred_element_type=f32)
    place = jnp.where((rank == column.astype(f32)) & (used > 0.0), 1.0, 0.0)
    chosen = place.T[:bins].astype(bf16)
    small[1].wait()
    dft[...] = jnp.concatenate(
        [jnp.dot(chosen, tab[r], preferred_element_type=f32) for r in range(2)], axis=0
    ).astype(bf16)

    def transform(c):
        fetch(c).wait()

        def step(p, carry):
            for pair in range(blocks // 2):
                y = [
                    jnp.dot(
                        dft[...],
                        series[
                            c,
                            b * NT : (b + 1) * NT,
                            pl.ds(pl.multiple_of(p * 2 * LANES, 2 * LANES), 2 * LANES),
                        ],
                        preferred_element_type=f32,
                    )
                    for b in (2 * pair, 2 * pair + 1)
                ]
                y = jnp.concatenate(y, axis=0).astype(bf16)
                rows = pl.ds(pair * 4 * bins, 4 * bins)
                stage[c, 2 * p, rows, :] = y[:, :LANES]
                stage[c, 2 * p + 1, rows, :] = y[:, LANES:]
            return carry

        lax.fori_loop(0, n // 2, step, 0)

    def exchange(c, off):
        peer = lax.rem(me + off, n)
        return pltpu.make_async_remote_copy(
            src_ref=stage.at[c, peer],
            dst_ref=recv.at[c, me],
            send_sem=send_sem.at[c, off],
            recv_sem=recv_sem.at[c, off],
            device_id=(peer, col),
            device_id_type=MESH,
        )

    transform(0)
    pl.semaphore_wait(barrier, 2 * n)
    for c in range(comps):
        if c > 0:
            transform(c)

        def begin(off, carry, c=c):
            exchange(c, off).start()
            return carry

        lax.fori_loop(1, n, begin, 0)

    for copy in small[2:]:
        copy.wait()
    width = -(-bins // GROUP) * GROUP
    shift = width - bins
    wide = (owners, total_slots)
    spread = jnp.where(
        lax.rem(iota((per_owner, total_slots), 1), per_owner)
        == iota((per_owner, total_slots), 0),
        1.0,
        0.0,
    )
    tiled = jnp.dot(
        slots[...].astype(f32).astype(bf16),
        spread.astype(bf16),
        preferred_element_type=f32,
    )
    own_row = iota(wide, 1) // per_owner == iota(wide, 0)
    slot_triad = jnp.sum(jnp.where(own_row, tiled, 0.0), axis=0, keepdims=True)
    holds = jnp.where(
        iota((count, total_slots), 0).astype(f32) == slot_triad, 1.0, 0.0
    ).astype(bf16)
    slot_freq = jnp.dot(
        (triads[...] + 1).astype(f32).astype(bf16), holds, preferred_element_type=f32
    )
    for role in range(3):
        named = jnp.where(
            iota((K, total_slots), 0).astype(f32) + 1.0 == slot_freq[role : role + 1, :],
            1.0,
            0.0,
        )
        for side in range(pick.shape[0]):
            spot = column.astype(f32) - float(side * shift)
            at_rank = jnp.where((rank == spot) & (used > 0.0), 1.0, 0.0)
            chosen_all = jnp.dot(
                at_rank.T.astype(bf16), named.astype(bf16), preferred_element_type=f32
            )
            pick[side, role * total_slots : (role + 1) * total_slots, :] = chosen_all.T[
                :, :width
            ].astype(bf16)

    w_row = weights[pl.ds(me, 1), :] * weight_scale

    def look_up(c, src, ref):
        for pair in range(blocks // 2):
            got = ref[c, src, pair * 4 * bins : (pair + 1) * 4 * bins, :]
            if bins % 16 != 0:
                got = got.astype(f32)
            re = [got[b * 2 * bins : b * 2 * bins + width] for b in range(2)]
            im = [got[(b + 1) * 2 * bins - width : (b + 1) * 2 * bins] for b in range(2)]
            if shift == 0:
                looked[...] = jnp.dot(
                    pick[0],
                    jnp.concatenate(re + im, axis=1).astype(bf16),
                    preferred_element_type=f32,
                )
            else:
                for side, values in enumerate((re, im)):
                    looked[:, side * 2 * LANES : (side + 1) * 2 * LANES] = jnp.dot(
                        pick[side],
                        jnp.concatenate(values, axis=1).astype(bf16),
                        preferred_element_type=f32,
                    )
            first = src * (blocks * GROUP) + pair * 2 * GROUP
            at = pl.ds(pl.multiple_of(first, 2 * GROUP), 2 * GROUP)
            at_imag = pl.ds(pl.multiple_of(NB * GROUP + first, 2 * GROUP), 2 * GROUP)

            def group(g, carry):
                def tile(role, q):
                    row = pl.multiple_of(role * total_slots + g * GROUP, GROUP)
                    return looked[pl.ds(row, GROUP), q * LANES : (q + 1) * LANES]

                re, im, c_re, c_im = [], [], [], []
                for b in range(2):
                    ar, ai = tile(0, b), tile(0, 2 + b)
                    br, bi = tile(1, b), tile(1, 2 + b)
                    re.append((ar * br - ai * bi) * w_row)
                    im.append((ar * bi + ai * br) * w_row)
                    c_re.append(tile(2, b))
                    c_im.append(tile(2, 2 + b))
                re, im, c_re, c_im = (
                    jnp.concatenate(v, axis=0) for v in (re, im, c_re, c_im)
                )
                prod[g, at, :LANES] = re.astype(bf16)
                prod[g, at, LANES:] = im.astype(bf16)
                third[g, at, :LANES] = c_re.astype(bf16)
                third[g, at, LANES:] = c_im.astype(bf16)
                third[g, at_imag, :LANES] = c_im.astype(bf16)
                third[g, at_imag, LANES:] = (-c_re).astype(bf16)
                return carry

            lax.fori_loop(0, groups, group, 0, unroll=4)

    def gram(g):
        return lax.dot_general(
            prod[g], third[g], (((1,), (1,)), ((), ())), preferred_element_type=f32
        )

    sub = iota((GROUP, LANES), 0)
    turn = lax.rem(sub - iota((GROUP, LANES), 1) + LANES, GROUP)
    low = lax.rem(iota((NB, LANES), 1), GROUP) < GROUP // 2

    def diagonal(total, side):
        octets = []
        for o in range(NB // GROUP):
            rows = []
            for b in range(GROUP):
                at = (o * GROUP + b) * GROUP
                rows.append(total[at : at + GROUP, side * LANES : (side + 1) * LANES])
            for k in (1, 2, 4):
                even, stay = (sub & k) == 0, (turn & k) == 0
                rows = [
                    jnp.where(
                        stay,
                        jnp.where(even, rows[i], rows[i + 1]),
                        pltpu.roll(jnp.where(even, rows[i + 1], rows[i]), k, 0),
                    )
                    for i in range(0, len(rows), 2)
                ]
            octets.append(rows[0])
        return jnp.concatenate(octets, axis=0)

    def partner(step):
        total, bit = 0, 1
        while bit < n:
            total = total + lax.rem(me // bit + step // bit, 2) * bit
            bit *= 2
        return total

    for c in range(comps):
        look_up(c, me, stage)

        def arrive(off, carry, c=c):
            exchange(c, off).wait_recv()
            look_up(c, lax.rem(me - off + n, n), recv)
            return carry

        lax.fori_loop(1, n, arrive, 0)
        if c < comps - 1:

            def grams(g, carry, c=c):
                if c == 0:
                    acc[g] = gram(g)
                else:
                    acc[g] += gram(g)
                return carry

            lax.fori_loop(0, groups, grams, 0, unroll=2)

    def finish(side, h):
        def owner(i, carry):
            g = i * halves + h
            total = acc[g] + gram(g)
            real, imag = diagonal(total, 0), diagonal(total, 1)
            tiles[0, side, i] = jnp.where(low, real, pltpu.roll(imag, GROUP // 2, 1))
            tiles[1, side, i] = jnp.where(
                low, pltpu.roll(real, LANES - GROUP // 2, 1), imag
            )
            return carry

        lax.fori_loop(0, owners, owner, 0, unroll=4)

    def swap(side):
        return pltpu.make_async_remote_copy(
            src_ref=tiles.at[1 - core, side],
            dst_ref=paired.at[side],
            send_sem=send_pair.at[side],
            recv_sem=recv_pair.at[side],
            device_id=sibling,
            device_id_type=MESH,
        )

    def deliver(side, i, h):
        return pltpu.make_async_remote_copy(
            src_ref=sums.at[side, i],
            dst_ref=land.at[me_at],
            send_sem=send_tile.at[side, i],
            recv_sem=recv_tile.at[me_at],
            device_id=(i, 2 * h + core),
            device_id_type=MESH,
        )

    for side, h in enumerate((1 - here, here)):
        finish(side, h)
        swap(side).start()

    for side, h in enumerate((1 - here, here)):
        swap(side).wait_recv()
        chip_sum = tiles[core, side] + paired[side]
        sums[side] = chip_sum.astype(bf16)
        if side == 1:
            paired[side] = chip_sum

        def give(step, carry, side=side, h=h):
            deliver(side, partner(n - 1 - step), h).start()
            return carry

        lax.fori_loop(0, n if side == 0 else n - 1, give, 0, unroll=True)

    def drain(off, carry):
        for c in range(comps):
            exchange(c, off).wait_send()
        return carry

    lax.fori_loop(1, n, drain, 0)
    for side in range(2):
        swap(side).wait_send()

    def landed(off):
        i, h = chip(off)
        return pltpu.make_async_remote_copy(
            src_ref=sums.at[0, i],
            dst_ref=land.at[2 * i + h],
            send_sem=send_tile.at[0, i],
            recv_sem=recv_tile.at[2 * i + h],
            device_id=(i, 2 * h + core),
            device_id_type=MESH,
        )

    def collect(off, carry):
        landed(off).wait_recv()
        return carry

    lax.fori_loop(1, 2 * n, collect, 0)
    total = paired[1, me]
    for off in range(1, 2 * n):
        total = total + land[lax.rem(me_at + off, 2 * n)].astype(f32)
    out[...] = total

    def sent(step, carry):
        deliver(0, step, 1 - here).wait_send()
        return carry

    def sent_near(off, carry):
        deliver(1, lax.rem(me + off, n), here).wait_send()
        return carry

    lax.fori_loop(0, n, sent, 0)
    lax.fori_loop(1, n, sent_near, 0)


def lean_tile(n, ns, bins, weight_scale, snap, table, weights, triads, slots):
    comps, times, cells = snap.shape
    owners, per_owner = slots.shape
    groups = owners * per_owner // GROUP
    rows = times // NT * 2 * bins
    width = -(-bins // GROUP) * GROUP
    vmem = pl.BlockSpec(memory_space=pltpu.VMEM)
    anywhere = pl.BlockSpec(memory_space=pl.ANY)
    sem = pltpu.SemaphoreType.DMA
    return pl.pallas_call(
        functools.partial(lean_kernel, n, ns, bins, weight_scale),
        out_shape=jax.ShapeDtypeStruct((NB, LANES), jnp.float32),
        in_specs=[anywhere] * 5,
        out_specs=vmem,
        scratch_shapes=[
            pltpu.VMEM((comps, times, cells), jnp.bfloat16),
            pltpu.VMEM((2, K, NT), jnp.bfloat16),
            pltpu.VMEM(weights.shape, jnp.float32),
            pltpu.VMEM(triads.shape, jnp.int32),
            pltpu.VMEM(slots.shape, jnp.int32),
            pltpu.VMEM((2 * bins, NT), jnp.bfloat16),
            pltpu.VMEM((1 if width == bins else 2, 3 * owners * per_owner, width), jnp.bfloat16),
            pltpu.VMEM((comps, n, rows, LANES), jnp.bfloat16),
            pltpu.VMEM((comps, n, rows, LANES), jnp.bfloat16),
            pltpu.VMEM((3 * owners * per_owner, 4 * LANES), jnp.float32),
            pltpu.VMEM((groups, NB * GROUP, 2 * LANES), jnp.bfloat16),
            pltpu.VMEM((groups, 2 * NB * GROUP, 2 * LANES), jnp.bfloat16),
            pltpu.VMEM((groups, NB * GROUP, 2 * LANES), jnp.float32),
            pltpu.VMEM((2, 2, n, NB, LANES), jnp.float32),
            pltpu.VMEM((2, n, NB, LANES), jnp.float32),
            pltpu.VMEM((2, n, NB, LANES), jnp.bfloat16),
            pltpu.VMEM((2 * n, NB, LANES), jnp.bfloat16),
            sem((comps + 4,)),
            sem((comps, n)),
            sem((comps, n)),
            sem((2,)),
            sem((2,)),
            sem((2, n)),
            sem((2 * n,)),
        ],
        compiler_params=pltpu.CompilerParams(
            collective_id=bins, has_side_effects=True, vmem_limit_bytes=60 * 1024 * 1024
        ),
    )(snap, table, weights, triads, slots)


def size_class(bins, triads, out):
    count = triads.shape[1]
    freq = lax.broadcasted_iota(jnp.int32, (K, count), 0)
    hit = (
        (freq == triads[0:1, :]) | (freq == triads[1:2, :]) | (freq == triads[2:3, :])
    )
    used = jnp.sum(jnp.max(jnp.where(hit, 1.0, 0.0), axis=1, keepdims=True))
    index = jnp.int32(0)
    for size in bins[:-1]:
        index += (used > size).astype(jnp.int32)
    out[0] = index


def lean(n, ns, snapshots, cell_weights, triads, owner_slots):
    times, comps, cells = snapshots.shape
    index = pl.pallas_call(
        functools.partial(size_class, BINS),
        out_shape=jax.ShapeDtypeStruct((1,), jnp.int32),
        in_specs=[pl.BlockSpec(memory_space=pltpu.VMEM)],
        out_specs=pl.BlockSpec(memory_space=pltpu.SMEM),
    )(triads.T)
    scale = 1.0 / math.sqrt(comps * cells * ns)
    tile = lax.switch(
        index[0],
        [functools.partial(lean_tile, n, ns, bins, scale) for bins in BINS],
        snapshots.transpose(1, 0, 2),
        jnp.asarray(spectral_table().reshape(K, 2, NT).transpose(1, 0, 2)),
        cell_weights.reshape(n, LANES),
        triads.T,
        owner_slots,
    )
    mine = owner_slots.shape[1] // ns
    return tile.reshape(NB, NB, 2, mine).transpose(3, 2, 0, 1).reshape(mine, 2 * NB * NB)


def shards(n, ns, snapshots, cell_weights, triads, owner_slots):
    times, comps, cells = snapshots.shape
    owners, slot_count = owner_slots.shape
    lean_slots = ns == 4 and slot_count == 2 * GROUP and owners == n
    if lean_slots and times % (2 * NT) == 0 and n & (n - 1) == 0:
        return lean(n, ns, snapshots, cell_weights, triads, owner_slots)
    weight_scale = 1.0 / math.sqrt(comps * cells * ns)
    vmem = pl.BlockSpec(memory_space=pltpu.VMEM)
    smem = pl.BlockSpec(memory_space=pltpu.SMEM)
    anywhere = pl.BlockSpec(memory_space=pl.ANY)
    sem = pltpu.SemaphoreType.DMA
    tile = pl.pallas_call(
        functools.partial(kernel, n, ns, weight_scale),
        out_shape=jax.ShapeDtypeStruct((NB, LANES), jnp.float32),
        in_specs=[anywhere, vmem, vmem, smem],
        out_specs=vmem,
        scratch_shapes=[
            pltpu.VMEM((comps, NB * NT, LANES), jnp.bfloat16),
            pltpu.VMEM((2 * K * NB, LANES), jnp.float32),
            pltpu.VMEM((K, 2 * NB, LANES), jnp.float32),
            pltpu.VMEM((K, 2 * NB, LANES), jnp.bfloat16),
            pltpu.VMEM((ns, n, NB, LANES), jnp.float32),
            pltpu.VMEM((ns - 1, n, NB, LANES), jnp.float32),
            pltpu.VMEM((n, NB, LANES), jnp.float32),
            pltpu.VMEM((n, NB, LANES), jnp.float32),
            sem((comps, n)),
            sem((comps, n)),
            sem((comps,)),
            sem((ns - 1,)),
            sem((ns - 1,)),
            sem((n,)),
            sem((n,)),
        ],
        compiler_params=pltpu.CompilerParams(
            collective_id=0, has_side_effects=True, vmem_limit_bytes=40 * 1024 * 1024
        ),
    )(
        snapshots.transpose(1, 0, 2),
        jnp.asarray(spectral_table()),
        cell_weights.reshape(n, LANES),
        jnp.take(triads.T, jnp.maximum(owner_slots, 0).reshape(-1), axis=1, mode="clip"),
    )
    mine = slot_count // ns
    flat = tile.reshape(NB, 2, mine, NB).transpose(2, 1, 0, 3).reshape(mine, 2 * NB * NB)
    my_slots = lax.dynamic_slice(
        owner_slots, (lax.axis_index("tm"), lax.axis_index("space") * mine), (1, mine)
    ).reshape(mine, 1)
    return jnp.where(my_slots >= 0, flat, 0.0)


def solution(mesh):
    placed = (P("tm", None, "space"), P("space"), P(), P())
    n, ns = mesh.shape["tm"], mesh.shape["space"]
    return jax.shard_map(
        functools.partial(shards, n, ns),
        mesh=mesh,
        in_specs=placed,
        out_specs=P(("tm", "space"), None),
        check_vma=False,
    )
```

```python
import functools
import math

import jax
import jax.numpy as jnp
import ml_dtypes
import numpy as np
from jax import lax
from jax.experimental import pallas as pl
from jax.experimental.pallas import tpu as pltpu
from jax.sharding import PartitionSpec as P

NB = 16
NT = 256
K = 128
GROUP = 8
LANES = 128
BINS = (92, 96, 100, 104, 112, K)
MESH = pl.DeviceIdType.MESH


def spectral_table():
    sample = np.arange(NT)
    freq_bins = np.arange(K)
    angles = 2.0 * math.pi / NT * (freq_bins[:, None] * sample[None, :] % NT)
    window = 0.5 - 0.5 * np.cos(2.0 * math.pi / NT * sample)
    scale = math.sqrt(8.0 / (3.0 * NT))
    rows = np.stack(
        [scale * window * np.cos(angles), -scale * window * np.sin(angles)], axis=1
    )
    return rows.reshape(2 * K, NT).astype(np.float32).astype(ml_dtypes.bfloat16)


def kernel(
    n,
    ns,
    weight_scale,
    snap,
    table,
    weights,
    freqs,
    out,
    recv,
    rows,
    spec,
    narrow,
    acc,
    part,
    summed,
    last,
    send_sem,
    recv_sem,
    own_sem,
    send1,
    recv1,
    send2,
    recv2,
):
    comps, times = snap.shape[0], snap.shape[1]
    me = lax.axis_index("tm")
    col = lax.axis_index("space")

    barrier = pltpu.get_barrier_semaphore()

    def greet_tm(off, carry):
        pl.semaphore_signal(
            barrier, inc=1, device_id=(lax.rem(me + off, n), col), device_id_type=MESH
        )
        return carry

    lax.fori_loop(1, n, greet_tm, 0)
    for off in range(1, ns):
        pl.semaphore_signal(
            barrier, inc=1, device_id=(me, lax.rem(col + off, ns)), device_id_type=MESH
        )
    pl.semaphore_wait(barrier, n - 1 + ns - 1)

    def exchange(c, off):
        peer = lax.rem(me + off, n)
        return pltpu.make_async_remote_copy(
            src_ref=snap.at[c, :, pl.ds(pl.multiple_of(peer * LANES, LANES), LANES)],
            dst_ref=recv.at[c, pl.ds(pl.multiple_of(me * times, 16), times), :],
            send_sem=send_sem.at[c, off],
            recv_sem=recv_sem.at[c, off],
            device_id=(peer, col),
            device_id_type=MESH,
        )

    def own(c):
        return pltpu.make_async_copy(
            snap.at[c, :, pl.ds(pl.multiple_of(me * LANES, LANES), LANES)],
            recv.at[c, pl.ds(pl.multiple_of(me * times, 16), times), :],
            own_sem.at[c],
        )

    for c in range(comps):

        def begin(off, carry, c=c):
            exchange(c, off).start()
            return carry

        lax.fori_loop(1, n, begin, 0)
        own(c).start()

    w_row = weights[pl.ds(me, 1), :] * weight_scale
    lane = lax.broadcasted_iota(jnp.int32, (2 * NB, 2 * LANES), 1)
    lane_group = lax.rem(lane, LANES) // NB
    low = lax.broadcasted_iota(jnp.int32, (NB, LANES), 1) < LANES // 2
    groups = freqs.shape[1] // GROUP
    per_owner = groups // n

    def dft(c, b):
        x = recv[c, pl.ds(pl.multiple_of(b * NT, NT), NT), :]
        y = jnp.dot(table[...], x, preferred_element_type=jnp.float32)
        rows[pl.ds(b, 2 * K, stride=NB), :] = y

    def regroup(k, carry):
        both = rows[pl.ds(pl.multiple_of(k * 2 * NB, 2 * NB), 2 * NB), :].astype(jnp.bfloat16)
        narrow[k] = both
        spec[k] = both.astype(jnp.float32)
        return carry

    def gram_group(c, g):
        owner = g // per_owner
        half = lax.rem(g, per_owner)
        prods, c_re, c_im = [], [], []
        for s in range(GROUP):
            place = g * GROUP + s
            a = spec[freqs[0, place]]
            b2 = spec[freqs[1, place]]
            c2 = narrow[freqs[2, place]]
            re = (a[:NB] * b2[:NB] - a[NB:] * b2[NB:]) * w_row
            im = (a[:NB] * b2[NB:] + a[NB:] * b2[:NB]) * w_row
            prods += [re.astype(jnp.bfloat16), im.astype(jnp.bfloat16)]
            c_re.append(c2[:NB])
            c_im.append(c2[NB:])
        left = jnp.concatenate(prods, axis=0)
        right = jnp.concatenate(c_re + c_im, axis=0)
        gram = lax.dot_general(
            left, right, (((1,), (1,)), ((), ())), preferred_element_type=jnp.float32
        )
        diag = gram[: 2 * NB]
        for s in range(1, GROUP):
            diag = jnp.where(lane_group == s, gram[2 * NB * s : 2 * NB * (s + 1)], diag)
        real = diag[:NB, :LANES] + diag[NB:, LANES:]
        imag = diag[:NB, LANES:] - diag[NB:, :LANES]
        half_turn = LANES // 2
        first = jnp.where(low, real, pltpu.roll(imag, half_turn, 1))
        second = jnp.where(low, pltpu.roll(real, half_turn, 1), imag)
        if c == 0:
            acc[2 * half, owner] = first
            acc[2 * half + 1, owner] = second
        else:
            acc[2 * half, owner] += first
            acc[2 * half + 1, owner] += second

    for c in range(comps):
        own(c).wait()
        if times % NT == 0:

            def transform(i, carry, c=c):
                dft(c, me * (times // NT) + i)
                return carry

            lax.fori_loop(0, times // NT, transform, 0)

            def arrive(off, carry, c=c):
                exchange(c, off).wait_recv()
                src = lax.rem(me - off + n, n)
                for i in range(times // NT):
                    dft(c, src * (times // NT) + i)
                return carry

            lax.fori_loop(1, n, arrive, 0)
        else:

            def arrive(off, carry, c=c):
                exchange(c, off).wait_recv()
                return carry

            lax.fori_loop(1, n, arrive, 0)

            def transform(b, carry, c=c):
                dft(c, b)
                return carry

            lax.fori_loop(0, NB, transform, 0)

        lax.fori_loop(0, K, regroup, 0, unroll=4)

        def grams(g, carry, c=c):
            gram_group(c, g)
            return carry

        lax.fori_loop(0, groups, grams, 0)

    def across(off):
        peer = lax.rem(col + off, ns)
        return pltpu.make_async_remote_copy(
            src_ref=acc.at[peer],
            dst_ref=part.at[off - 1],
            send_sem=send1.at[off - 1],
            recv_sem=recv1.at[off - 1],
            device_id=(me, peer),
            device_id_type=MESH,
        )

    for off in range(1, ns):
        across(off).start()
    for off in range(1, ns):
        across(off).wait_recv()
    total = acc[col]
    for off in range(1, ns):
        total = total + part[off - 1]
    summed[...] = total

    def along(off):
        peer = lax.rem(me + off, n)
        return pltpu.make_async_remote_copy(
            src_ref=summed.at[peer],
            dst_ref=last.at[off],
            send_sem=send2.at[off],
            recv_sem=recv2.at[off],
            device_id=(peer, col),
            device_id_type=MESH,
        )

    def begin2(off, carry):
        along(off).start()
        return carry

    lax.fori_loop(1, n, begin2, 0)

    def add2(off, total):
        along(off).wait_recv()
        return total + last[off]

    out[...] = lax.fori_loop(1, n, add2, summed[me])

    for off in range(1, ns):
        across(off).wait_send()

    def drain(off, carry):
        for c in range(comps):
            exchange(c, off).wait_send()
        along(off).wait_send()
        return carry

    lax.fori_loop(1, n, drain, 0)


def lean_kernel(
    n,
    ns,
    bins,
    weight_scale,
    snap,
    table,
    weights_at,
    triads_at,
    slots_at,
    out,
    series,
    tab,
    weights,
    triads,
    slots,
    dft,
    pick,
    stage,
    recv,
    looked,
    prod,
    third,
    acc,
    tiles,
    paired,
    sums,
    land,
    load_sem,
    send_sem,
    recv_sem,
    send_pair,
    recv_pair,
    send_tile,
    recv_tile,
):
    comps, times, cells = series.shape
    blocks = times // NT
    count = triads.shape[1]
    owners, per_owner = slots.shape
    total_slots = owners * per_owner
    groups = total_slots // GROUP
    halves = per_owner // GROUP
    me = lax.axis_index("tm")
    col = lax.axis_index("space")
    f32, bf16 = jnp.float32, jnp.bfloat16

    def iota(shape, axis):
        return lax.broadcasted_iota(jnp.int32, shape, axis)

    core, here = lax.rem(col, 2), col // 2
    sibling = (me, 2 * here + 1 - core)
    me_at = 2 * me + here

    def chip(off):
        other = lax.rem(me_at + off, 2 * n)
        return other // 2, lax.rem(other, 2)

    barrier = pltpu.get_barrier_semaphore()

    def greet(off, carry):
        i, h = chip(off)
        pl.semaphore_signal(
            barrier, inc=1, device_id=(i, 2 * h + core), device_id_type=MESH
        )
        return carry

    pl.semaphore_signal(barrier, inc=1, device_id=sibling, device_id_type=MESH)
    lax.fori_loop(1, 2 * n, greet, 0)

    small = [
        pltpu.make_async_copy(source, target, load_sem.at[comps + i])
        for i, (source, target) in enumerate(
            ((triads_at, triads), (table, tab), (slots_at, slots), (weights_at, weights))
        )
    ]

    def fetch(c):
        return pltpu.make_async_copy(snap.at[c], series.at[c], load_sem.at[c])

    for copy in small:
        copy.start()
    for c in range(comps):
        fetch(c).start()
    small[0].wait()

    freq = iota((K, count), 0)
    hit = (
        (freq == triads[0:1, :]) | (freq == triads[1:2, :]) | (freq == triads[2:3, :])
    )
    used = jnp.max(jnp.where(hit, 1.0, 0.0), axis=1, keepdims=True)
    used = jnp.broadcast_to(used, (K, K))
    column = iota((K, K), 1)
    below = jnp.where(column < iota((K, K), 0), 1.0, 0.0)
    rank = jnp.dot(below.astype(bf16), used.astype(bf16), preferred_element_type=f32)
    place = jnp.where((rank == column.astype(f32)) & (used > 0.0), 1.0, 0.0)
    chosen = place.T[:bins].astype(bf16)
    small[1].wait()
    dft[...] = jnp.concatenate(
        [jnp.dot(chosen, tab[r], preferred_element_type=f32) for r in range(2)], axis=0
    ).astype(bf16)

    def transform(c):
        fetch(c).wait()

        def step(p, carry):
            for pair in range(blocks // 2):
                y = [
                    jnp.dot(
                        dft[...],
                        series[
                            c,
                            b * NT : (b + 1) * NT,
                            pl.ds(pl.multiple_of(p * 2 * LANES, 2 * LANES), 2 * LANES),
                        ],
                        preferred_element_type=f32,
                    )
                    for b in (2 * pair, 2 * pair + 1)
                ]
                y = jnp.concatenate(y, axis=0).astype(bf16)
                rows = pl.ds(pair * 4 * bins, 4 * bins)
                stage[c, 2 * p, rows, :] = y[:, :LANES]
                stage[c, 2 * p + 1, rows, :] = y[:, LANES:]
            return carry

        lax.fori_loop(0, n // 2, step, 0)

    def exchange(c, off):
        peer = lax.rem(me + off, n)
        return pltpu.make_async_remote_copy(
            src_ref=stage.at[c, peer],
            dst_ref=recv.at[c, me],
            send_sem=send_sem.at[c, off],
            recv_sem=recv_sem.at[c, off],
            device_id=(peer, col),
            device_id_type=MESH,
        )

    transform(0)
    pl.semaphore_wait(barrier, 2 * n)
    for c in range(comps):
        if c > 0:
            transform(c)

        def begin(off, carry, c=c):
            exchange(c, off).start()
            return carry

        lax.fori_loop(1, n, begin, 0)

    for copy in small[2:]:
        copy.wait()
    width = -(-bins // GROUP) * GROUP
    shift = width - bins
    wide = (owners, total_slots)
    spread = jnp.where(
        lax.rem(iota((per_owner, total_slots), 1), per_owner)
        == iota((per_owner, total_slots), 0),
        1.0,
        0.0,
    )
    tiled = jnp.dot(
        slots[...].astype(f32).astype(bf16),
        spread.astype(bf16),
        preferred_element_type=f32,
    )
    own_row = iota(wide, 1) // per_owner == iota(wide, 0)
    slot_triad = jnp.sum(jnp.where(own_row, tiled, 0.0), axis=0, keepdims=True)
    holds = jnp.where(
        iota((count, total_slots), 0).astype(f32) == slot_triad, 1.0, 0.0
    ).astype(bf16)
    slot_freq = jnp.dot(
        (triads[...] + 1).astype(f32).astype(bf16), holds, preferred_element_type=f32
    )
    found = [[], []]
    for role in range(3):
        named = jnp.where(
            iota((K, total_slots), 0).astype(f32) + 1.0 == slot_freq[role : role + 1, :],
            1.0,
            0.0,
        )
        for side in range(pick.shape[0]):
            spot = column.astype(f32) - float(side * shift)
            at_rank = jnp.where((rank == spot) & (used > 0.0), 1.0, 0.0)
            chosen_all = jnp.dot(
                at_rank.T.astype(bf16), named.astype(bf16), preferred_element_type=f32
            )
            found[side].append(chosen_all.T[:, :width])
    for side in range(pick.shape[0]):
        pick[side] = jnp.concatenate(
            [
                found[side][role][g * GROUP : (g + 1) * GROUP]
                for g in range(groups)
                for role in range(3)
            ],
            axis=0,
        ).astype(bf16)

    w_row = weights[pl.ds(me, 1), :] * weight_scale

    def look_up(c, src, ref):
        for pair in range(blocks // 2):
            got = ref[c, src, pair * 4 * bins : (pair + 1) * 4 * bins, :]
            if bins % 16 != 0:
                got = got.astype(f32)
            re = [got[b * 2 * bins : b * 2 * bins + width] for b in range(2)]
            im = [got[(b + 1) * 2 * bins - width : (b + 1) * 2 * bins] for b in range(2)]
            if shift == 0:
                looked[...] = jnp.dot(
                    pick[0],
                    jnp.concatenate(re + im, axis=1).astype(bf16),
                    preferred_element_type=f32,
                )
            else:
                for side, values in enumerate((re, im)):
                    looked[:, side * 2 * LANES : (side + 1) * 2 * LANES] = jnp.dot(
                        pick[side],
                        jnp.concatenate(values, axis=1).astype(bf16),
                        preferred_element_type=f32,
                    )
            first = src * (blocks * GROUP) + pair * 2 * GROUP
            at = pl.ds(pl.multiple_of(first, 2 * GROUP), 2 * GROUP)
            at_imag = pl.ds(pl.multiple_of(NB * GROUP + first, 2 * GROUP), 2 * GROUP)

            def group(g, carry):
                def tile(role, q):
                    row = pl.multiple_of((3 * g + role) * GROUP, GROUP)
                    return looked[pl.ds(row, GROUP), q * LANES : (q + 1) * LANES]

                re, im, c_re, c_im = [], [], [], []
                for b in range(2):
                    ar, ai = tile(0, b), tile(0, 2 + b)
                    br, bi = tile(1, b), tile(1, 2 + b)
                    re.append((ar * br - ai * bi) * w_row)
                    im.append((ar * bi + ai * br) * w_row)
                    c_re.append(tile(2, b))
                    c_im.append(tile(2, 2 + b))
                re, im, c_re, c_im = (
                    jnp.concatenate(v, axis=0) for v in (re, im, c_re, c_im)
                )
                prod[g, at, :LANES] = re.astype(bf16)
                prod[g, at, LANES:] = im.astype(bf16)
                third[g, at, :LANES] = c_re.astype(bf16)
                third[g, at, LANES:] = c_im.astype(bf16)
                third[g, at_imag, :LANES] = c_im.astype(bf16)
                third[g, at_imag, LANES:] = (-c_re).astype(bf16)
                return carry

            lax.fori_loop(0, groups, group, 0, unroll=True)

    def gram(g):
        return lax.dot_general(
            prod[g], third[g], (((1,), (1,)), ((), ())), preferred_element_type=f32
        )

    sub = iota((GROUP, LANES), 0)
    turn = lax.rem(sub - iota((GROUP, LANES), 1) + LANES, GROUP)
    low = lax.rem(iota((NB, LANES), 1), GROUP) < GROUP // 2

    def diagonal(total, side):
        octets = []
        for o in range(NB // GROUP):
            rows = []
            for b in range(GROUP):
                at = (o * GROUP + b) * GROUP
                rows.append(total[at : at + GROUP, side * LANES : (side + 1) * LANES])
            for k in (1, 2, 4):
                even, stay = (sub & k) == 0, (turn & k) == 0
                rows = [
                    jnp.where(
                        stay,
                        jnp.where(even, rows[i], rows[i + 1]),
                        pltpu.roll(jnp.where(even, rows[i + 1], rows[i]), k, 0),
                    )
                    for i in range(0, len(rows), 2)
                ]
            octets.append(rows[0])
        return jnp.concatenate(octets, axis=0)

    def partner(step):
        total, bit = 0, 1
        while bit < n:
            total = total + lax.rem(me // bit + step // bit, 2) * bit
            bit *= 2
        return total

    half = owners // 2

    def fold(side, first, past, with_acc, with_tiles):
        def tile(at, carry):
            i, h = partner(n - 1 - side * half - at // 2), lax.rem(at, 2)
            g = i * halves + h
            total = acc[g] + gram(g) if with_acc else gram(g)
            real, imag = diagonal(total, 0), diagonal(total, 1)
            both = (
                jnp.where(low, real, pltpu.roll(imag, GROUP // 2, 1)),
                jnp.where(low, pltpu.roll(real, LANES - GROUP // 2, 1), imag),
            )
            for q in range(2):
                before = tiles[q, side, at] if with_tiles else 0.0
                tiles[q, side, at] = before + both[q]
            return carry

        lax.fori_loop(first, past, tile, 0, unroll=True)

    def finish(side, first, past):
        fold(side, first, past, False, comps > 1)

    for c in range(comps):
        look_up(c, me, stage)

        def arrive(off, carry, c=c):
            exchange(c, off).wait_recv()
            look_up(c, lax.rem(me - off + n, n), recv)
            return carry

        lax.fori_loop(1, n, arrive, 0)
        if c < comps - 2:

            def grams(g, carry, c=c):
                acc[g] = gram(g) if c == 0 else acc[g] + gram(g)
                return carry

            lax.fori_loop(0, groups, grams, 0, unroll=2)
        elif c == comps - 2:
            for side in range(2):
                fold(side, 0, n, c > 0, False)

    def swap(side):
        return pltpu.make_async_remote_copy(
            src_ref=tiles.at[1 - core, side],
            dst_ref=paired.at[side],
            send_sem=send_pair.at[side],
            recv_sem=recv_pair.at[side],
            device_id=sibling,
            device_id_type=MESH,
        )

    def deliver(side, step, h):
        return pltpu.make_async_remote_copy(
            src_ref=sums.at[side, 2 * step + h],
            dst_ref=land.at[me_at],
            send_sem=send_tile.at[side, 2 * step + h],
            recv_sem=recv_tile.at[me_at],
            device_id=(partner(n - 1 - side * half - step), 2 * h + core),
            device_id_type=MESH,
        )

    def pass_on(side):
        swap(side).wait_recv()
        chip_sum = tiles[core, side] + paired[side]
        sums[side] = chip_sum.astype(bf16)
        if side == 1:
            paired[side] = chip_sum
        for step in range(half):
            deliver(side, step, 1 - here).start()
            if side * half + step < n - 1:
                deliver(side, step, here).start()

    finish(0, 0, n)
    swap(0).start()
    finish(1, 0, 4)
    pass_on(0)
    finish(1, 4, n)
    swap(1).start()
    pass_on(1)

    def drain(off, carry):
        for c in range(comps):
            exchange(c, off).wait_send()
        return carry

    lax.fori_loop(1, n, drain, 0)
    for side in range(2):
        swap(side).wait_send()

    def landed(off):
        i, h = chip(off)
        return pltpu.make_async_remote_copy(
            src_ref=sums.at[0, 0],
            dst_ref=land.at[2 * i + h],
            send_sem=send_tile.at[0, 0],
            recv_sem=recv_tile.at[2 * i + h],
            device_id=(i, 2 * h + core),
            device_id_type=MESH,
        )

    def collect(off, carry):
        landed(off).wait_recv()
        return carry

    lax.fori_loop(1, 2 * n, collect, 0)
    total = paired[1, n - 2 + here]
    for off in range(1, 2 * n):
        total = total + land[lax.rem(me_at + off, 2 * n)].astype(f32)
    out[...] = total

    for side in range(2):
        for step in range(half):
            deliver(side, step, 1 - here).wait_send()
            if side * half + step < n - 1:
                deliver(side, step, here).wait_send()


def lean_tile(n, ns, bins, weight_scale, snap, table, weights, triads, slots):
    comps, times, cells = snap.shape
    owners, per_owner = slots.shape
    groups = owners * per_owner // GROUP
    rows = times // NT * 2 * bins
    width = -(-bins // GROUP) * GROUP
    vmem = pl.BlockSpec(memory_space=pltpu.VMEM)
    anywhere = pl.BlockSpec(memory_space=pl.ANY)
    sem = pltpu.SemaphoreType.DMA
    return pl.pallas_call(
        functools.partial(lean_kernel, n, ns, bins, weight_scale),
        out_shape=jax.ShapeDtypeStruct((NB, LANES), jnp.float32),
        in_specs=[anywhere] * 5,
        out_specs=vmem,
        scratch_shapes=[
            pltpu.VMEM((comps, times, cells), jnp.bfloat16),
            pltpu.VMEM((2, K, NT), jnp.bfloat16),
            pltpu.VMEM(weights.shape, jnp.float32),
            pltpu.VMEM(triads.shape, jnp.int32),
            pltpu.VMEM(slots.shape, jnp.int32),
            pltpu.VMEM((2 * bins, NT), jnp.bfloat16),
            pltpu.VMEM((1 if width == bins else 2, 3 * owners * per_owner, width), jnp.bfloat16),
            pltpu.VMEM((comps, n, rows, LANES), jnp.bfloat16),
            pltpu.VMEM((comps, n, rows, LANES), jnp.bfloat16),
            pltpu.VMEM((3 * owners * per_owner, 4 * LANES), jnp.float32),
            pltpu.VMEM((groups, NB * GROUP, 2 * LANES), jnp.bfloat16),
            pltpu.VMEM((groups, 2 * NB * GROUP, 2 * LANES), jnp.bfloat16),
            pltpu.VMEM((groups, NB * GROUP, 2 * LANES), jnp.float32),
            pltpu.VMEM((2, 2, n, NB, LANES), jnp.float32),
            pltpu.VMEM((2, n, NB, LANES), jnp.float32),
            pltpu.VMEM((2, n, NB, LANES), jnp.bfloat16),
            pltpu.VMEM((2 * n, NB, LANES), jnp.bfloat16),
            sem((comps + 4,)),
            sem((comps, n)),
            sem((comps, n)),
            sem((2,)),
            sem((2,)),
            sem((2, n)),
            sem((2 * n,)),
        ],
        compiler_params=pltpu.CompilerParams(
            collective_id=bins, has_side_effects=True, vmem_limit_bytes=60 * 1024 * 1024
        ),
    )(snap, table, weights, triads, slots)


def size_class(bins, triads, out):
    count = triads.shape[1]
    freq = lax.broadcasted_iota(jnp.int32, (K, count), 0)
    hit = (
        (freq == triads[0:1, :]) | (freq == triads[1:2, :]) | (freq == triads[2:3, :])
    )
    used = jnp.sum(jnp.max(jnp.where(hit, 1.0, 0.0), axis=1, keepdims=True))
    index = jnp.int32(0)
    for size in bins[:-1]:
        index += (used > size).astype(jnp.int32)
    out[0] = index


def lean(n, ns, snapshots, cell_weights, triads, owner_slots):
    times, comps, cells = snapshots.shape
    index = pl.pallas_call(
        functools.partial(size_class, BINS),
        out_shape=jax.ShapeDtypeStruct((1,), jnp.int32),
        in_specs=[pl.BlockSpec(memory_space=pltpu.VMEM)],
        out_specs=pl.BlockSpec(memory_space=pltpu.SMEM),
    )(triads.T)
    scale = 1.0 / math.sqrt(comps * cells * ns)
    tile = lax.switch(
        index[0],
        [functools.partial(lean_tile, n, ns, bins, scale) for bins in BINS],
        snapshots.transpose(1, 0, 2),
        jnp.asarray(spectral_table().reshape(K, 2, NT).transpose(1, 0, 2)),
        cell_weights.reshape(n, LANES),
        triads.T,
        owner_slots,
    )
    mine = owner_slots.shape[1] // ns
    return tile.reshape(NB, NB, 2, mine).transpose(3, 2, 0, 1).reshape(mine, 2 * NB * NB)


def shards(n, ns, snapshots, cell_weights, triads, owner_slots):
    times, comps, cells = snapshots.shape
    owners, slot_count = owner_slots.shape
    lean_slots = ns == 4 and slot_count == 2 * GROUP and owners == n
    if lean_slots and times % (2 * NT) == 0 and n & (n - 1) == 0:
        return lean(n, ns, snapshots, cell_weights, triads, owner_slots)
    weight_scale = 1.0 / math.sqrt(comps * cells * ns)
    vmem = pl.BlockSpec(memory_space=pltpu.VMEM)
    smem = pl.BlockSpec(memory_space=pltpu.SMEM)
    anywhere = pl.BlockSpec(memory_space=pl.ANY)
    sem = pltpu.SemaphoreType.DMA
    tile = pl.pallas_call(
        functools.partial(kernel, n, ns, weight_scale),
        out_shape=jax.ShapeDtypeStruct((NB, LANES), jnp.float32),
        in_specs=[anywhere, vmem, vmem, smem],
        out_specs=vmem,
        scratch_shapes=[
            pltpu.VMEM((comps, NB * NT, LANES), jnp.bfloat16),
            pltpu.VMEM((2 * K * NB, LANES), jnp.float32),
            pltpu.VMEM((K, 2 * NB, LANES), jnp.float32),
            pltpu.VMEM((K, 2 * NB, LANES), jnp.bfloat16),
            pltpu.VMEM((ns, n, NB, LANES), jnp.float32),
            pltpu.VMEM((ns - 1, n, NB, LANES), jnp.float32),
            pltpu.VMEM((n, NB, LANES), jnp.float32),
            pltpu.VMEM((n, NB, LANES), jnp.float32),
            sem((comps, n)),
            sem((comps, n)),
            sem((comps,)),
            sem((ns - 1,)),
            sem((ns - 1,)),
            sem((n,)),
            sem((n,)),
        ],
        compiler_params=pltpu.CompilerParams(
            collective_id=0, has_side_effects=True, vmem_limit_bytes=40 * 1024 * 1024
        ),
    )(
        snapshots.transpose(1, 0, 2),
        jnp.asarray(spectral_table()),
        cell_weights.reshape(n, LANES),
        jnp.take(triads.T, jnp.maximum(owner_slots, 0).reshape(-1), axis=1, mode="clip"),
    )
    mine = slot_count // ns
    flat = tile.reshape(NB, 2, mine, NB).transpose(2, 1, 0, 3).reshape(mine, 2 * NB * NB)
    my_slots = lax.dynamic_slice(
        owner_slots, (lax.axis_index("tm"), lax.axis_index("space") * mine), (1, mine)
    ).reshape(mine, 1)
    return jnp.where(my_slots >= 0, flat, 0.0)


def solution(mesh):
    placed = (P("tm", None, "space"), P("space"), P(), P())
    n, ns = mesh.shape["tm"], mesh.shape["space"]
    return jax.shard_map(
        functools.partial(shards, n, ns),
        mesh=mesh,
        in_specs=placed,
        out_specs=P(("tm", "space"), None),
        check_vma=False,
    )
```

```python
import functools
import math

import jax
import jax.numpy as jnp
import ml_dtypes
import numpy as np
from jax import lax
from jax.experimental import pallas as pl
from jax.experimental.pallas import tpu as pltpu
from jax.sharding import PartitionSpec as P

NB = 16
NT = 256
K = 128
GROUP = 8
LANES = 128
BINS = (92, 94, 96, 98, 100, 102, 104, 108, K)
MESH = pl.DeviceIdType.MESH


def spectral_table():
    sample = np.arange(NT)
    freq_bins = np.arange(K)
    angles = 2.0 * math.pi / NT * (freq_bins[:, None] * sample[None, :] % NT)
    window = 0.5 - 0.5 * np.cos(2.0 * math.pi / NT * sample)
    scale = math.sqrt(8.0 / (3.0 * NT))
    rows = np.stack(
        [scale * window * np.cos(angles), -scale * window * np.sin(angles)], axis=1
    )
    return rows.reshape(2 * K, NT).astype(np.float32).astype(ml_dtypes.bfloat16)


def kernel(
    n,
    ns,
    weight_scale,
    snap,
    table,
    weights,
    freqs,
    out,
    recv,
    rows,
    spec,
    narrow,
    acc,
    part,
    summed,
    last,
    send_sem,
    recv_sem,
    own_sem,
    send1,
    recv1,
    send2,
    recv2,
):
    comps, times = snap.shape[0], snap.shape[1]
    me = lax.axis_index("tm")
    col = lax.axis_index("space")

    barrier = pltpu.get_barrier_semaphore()

    def greet_tm(off, carry):
        pl.semaphore_signal(
            barrier, inc=1, device_id=(lax.rem(me + off, n), col), device_id_type=MESH
        )
        return carry

    lax.fori_loop(1, n, greet_tm, 0)
    for off in range(1, ns):
        pl.semaphore_signal(
            barrier, inc=1, device_id=(me, lax.rem(col + off, ns)), device_id_type=MESH
        )
    pl.semaphore_wait(barrier, n - 1 + ns - 1)

    def exchange(c, off):
        peer = lax.rem(me + off, n)
        return pltpu.make_async_remote_copy(
            src_ref=snap.at[c, :, pl.ds(pl.multiple_of(peer * LANES, LANES), LANES)],
            dst_ref=recv.at[c, pl.ds(pl.multiple_of(me * times, 16), times), :],
            send_sem=send_sem.at[c, off],
            recv_sem=recv_sem.at[c, off],
            device_id=(peer, col),
            device_id_type=MESH,
        )

    def own(c):
        return pltpu.make_async_copy(
            snap.at[c, :, pl.ds(pl.multiple_of(me * LANES, LANES), LANES)],
            recv.at[c, pl.ds(pl.multiple_of(me * times, 16), times), :],
            own_sem.at[c],
        )

    for c in range(comps):

        def begin(off, carry, c=c):
            exchange(c, off).start()
            return carry

        lax.fori_loop(1, n, begin, 0)
        own(c).start()

    w_row = weights[pl.ds(me, 1), :] * weight_scale
    lane = lax.broadcasted_iota(jnp.int32, (2 * NB, 2 * LANES), 1)
    lane_group = lax.rem(lane, LANES) // NB
    low = lax.broadcasted_iota(jnp.int32, (NB, LANES), 1) < LANES // 2
    groups = freqs.shape[1] // GROUP
    per_owner = groups // n

    def dft(c, b):
        x = recv[c, pl.ds(pl.multiple_of(b * NT, NT), NT), :]
        y = jnp.dot(table[...], x, preferred_element_type=jnp.float32)
        rows[pl.ds(b, 2 * K, stride=NB), :] = y

    def regroup(k, carry):
        both = rows[pl.ds(pl.multiple_of(k * 2 * NB, 2 * NB), 2 * NB), :].astype(jnp.bfloat16)
        narrow[k] = both
        spec[k] = both.astype(jnp.float32)
        return carry

    def gram_group(c, g):
        owner = g // per_owner
        half = lax.rem(g, per_owner)
        prods, c_re, c_im = [], [], []
        for s in range(GROUP):
            place = g * GROUP + s
            a = spec[freqs[0, place]]
            b2 = spec[freqs[1, place]]
            c2 = narrow[freqs[2, place]]
            re = (a[:NB] * b2[:NB] - a[NB:] * b2[NB:]) * w_row
            im = (a[:NB] * b2[NB:] + a[NB:] * b2[:NB]) * w_row
            prods += [re.astype(jnp.bfloat16), im.astype(jnp.bfloat16)]
            c_re.append(c2[:NB])
            c_im.append(c2[NB:])
        left = jnp.concatenate(prods, axis=0)
        right = jnp.concatenate(c_re + c_im, axis=0)
        gram = lax.dot_general(
            left, right, (((1,), (1,)), ((), ())), preferred_element_type=jnp.float32
        )
        diag = gram[: 2 * NB]
        for s in range(1, GROUP):
            diag = jnp.where(lane_group == s, gram[2 * NB * s : 2 * NB * (s + 1)], diag)
        real = diag[:NB, :LANES] + diag[NB:, LANES:]
        imag = diag[:NB, LANES:] - diag[NB:, :LANES]
        half_turn = LANES // 2
        first = jnp.where(low, real, pltpu.roll(imag, half_turn, 1))
        second = jnp.where(low, pltpu.roll(real, half_turn, 1), imag)
        if c == 0:
            acc[2 * half, owner] = first
            acc[2 * half + 1, owner] = second
        else:
            acc[2 * half, owner] += first
            acc[2 * half + 1, owner] += second

    for c in range(comps):
        own(c).wait()
        if times % NT == 0:

            def transform(i, carry, c=c):
                dft(c, me * (times // NT) + i)
                return carry

            lax.fori_loop(0, times // NT, transform, 0)

            def arrive(off, carry, c=c):
                exchange(c, off).wait_recv()
                src = lax.rem(me - off + n, n)
                for i in range(times // NT):
                    dft(c, src * (times // NT) + i)
                return carry

            lax.fori_loop(1, n, arrive, 0)
        else:

            def arrive(off, carry, c=c):
                exchange(c, off).wait_recv()
                return carry

            lax.fori_loop(1, n, arrive, 0)

            def transform(b, carry, c=c):
                dft(c, b)
                return carry

            lax.fori_loop(0, NB, transform, 0)

        lax.fori_loop(0, K, regroup, 0, unroll=4)

        def grams(g, carry, c=c):
            gram_group(c, g)
            return carry

        lax.fori_loop(0, groups, grams, 0)

    def across(off):
        peer = lax.rem(col + off, ns)
        return pltpu.make_async_remote_copy(
            src_ref=acc.at[peer],
            dst_ref=part.at[off - 1],
            send_sem=send1.at[off - 1],
            recv_sem=recv1.at[off - 1],
            device_id=(me, peer),
            device_id_type=MESH,
        )

    for off in range(1, ns):
        across(off).start()
    for off in range(1, ns):
        across(off).wait_recv()
    total = acc[col]
    for off in range(1, ns):
        total = total + part[off - 1]
    summed[...] = total

    def along(off):
        peer = lax.rem(me + off, n)
        return pltpu.make_async_remote_copy(
            src_ref=summed.at[peer],
            dst_ref=last.at[off],
            send_sem=send2.at[off],
            recv_sem=recv2.at[off],
            device_id=(peer, col),
            device_id_type=MESH,
        )

    def begin2(off, carry):
        along(off).start()
        return carry

    lax.fori_loop(1, n, begin2, 0)

    def add2(off, total):
        along(off).wait_recv()
        return total + last[off]

    out[...] = lax.fori_loop(1, n, add2, summed[me])

    for off in range(1, ns):
        across(off).wait_send()

    def drain(off, carry):
        for c in range(comps):
            exchange(c, off).wait_send()
        along(off).wait_send()
        return carry

    lax.fori_loop(1, n, drain, 0)


def windows(bins):
    starts = [q * bins // GROUP * GROUP for q in range(4)]
    width = max(
        -(-(q * bins - start + bins) // GROUP) * GROUP for q, start in enumerate(starts)
    )
    starts = [min(start, 4 * bins - width) for start in starts]
    return width, starts, [q * bins - start for q, start in enumerate(starts)]


def lean_kernel(
    n,
    ns,
    bins,
    weight_scale,
    snap,
    table,
    weights_at,
    triads_at,
    slots_at,
    out,
    series,
    tab,
    weights,
    triads,
    slots,
    dft,
    pick,
    stage,
    recv,
    looked,
    prod,
    third,
    acc,
    tiles,
    paired,
    sums,
    land,
    load_sem,
    send_sem,
    recv_sem,
    send_pair,
    recv_pair,
    send_tile,
    recv_tile,
):
    comps, times, cells = series.shape
    count = triads.shape[1]
    owners, per_owner = slots.shape
    total_slots = owners * per_owner
    groups = total_slots // GROUP
    halves = per_owner // GROUP
    me = lax.axis_index("tm")
    col = lax.axis_index("space")
    f32, bf16 = jnp.float32, jnp.bfloat16

    def iota(shape, axis):
        return lax.broadcasted_iota(jnp.int32, shape, axis)

    core, here = lax.rem(col, 2), col // 2
    sibling = (me, 2 * here + 1 - core)
    me_at = 2 * me + here

    def chip(off):
        other = lax.rem(me_at + off, 2 * n)
        return other // 2, lax.rem(other, 2)

    barrier = pltpu.get_barrier_semaphore()

    def greet(off, carry):
        i, h = chip(off)
        pl.semaphore_signal(
            barrier, inc=1, device_id=(i, 2 * h + core), device_id_type=MESH
        )
        return carry

    pl.semaphore_signal(barrier, inc=1, device_id=sibling, device_id_type=MESH)
    lax.fori_loop(1, 2 * n, greet, 0)

    small = [
        pltpu.make_async_copy(source, target, load_sem.at[comps + i])
        for i, (source, target) in enumerate(
            ((triads_at, triads), (table, tab), (slots_at, slots), (weights_at, weights))
        )
    ]

    def fetch(c):
        return pltpu.make_async_copy(snap.at[c], series.at[c], load_sem.at[c])

    for copy in small:
        copy.start()
    for c in range(comps):
        fetch(c).start()
    small[0].wait()

    freq = iota((K, count), 0)
    hit = (
        (freq == triads[0:1, :]) | (freq == triads[1:2, :]) | (freq == triads[2:3, :])
    )
    used = jnp.max(jnp.where(hit, 1.0, 0.0), axis=1, keepdims=True)
    used = jnp.broadcast_to(used, (K, K))
    column = iota((K, K), 1)
    below = jnp.where(column < iota((K, K), 0), 1.0, 0.0)
    rank = jnp.dot(below.astype(bf16), used.astype(bf16), preferred_element_type=f32)
    rank_row, used_row = rank.T[0:1], used.T[0:1]
    small[1].wait()
    late = 2 * bins % GROUP
    for b in range(2):
        at = iota((dft.shape[1], K), 0).astype(f32) - float(b * late)
        halves_of = [
            jnp.where((at - float(r * bins) == rank_row) & (used_row > 0.0), 1.0, 0.0)
            for r in range(2)
        ]
        dft[b] = sum(
            jnp.dot(pick_rows.astype(bf16), tab[r], preferred_element_type=f32)
            for r, pick_rows in enumerate(halves_of)
        ).astype(bf16)

    def transform(c):
        fetch(c).wait()

        def step(p, carry):
            first, second = [
                jnp.dot(
                    dft[b],
                    series[
                        c,
                        b * NT : (b + 1) * NT,
                        pl.ds(pl.multiple_of(p * 2 * LANES, 2 * LANES), 2 * LANES),
                    ],
                    preferred_element_type=f32,
                )
                for b in range(2)
            ]
            if late == 0:
                pieces = [first, second]
            else:
                end = 2 * bins - late
                pieces = [first[:end], first[end:] + second[:GROUP], second[GROUP:]]
            y = jnp.concatenate(pieces, axis=0).astype(bf16)
            stage[c, 2 * p] = y[:, :LANES]
            stage[c, 2 * p + 1] = y[:, LANES:]
            return carry

        lax.fori_loop(0, n // 2, step, 0)

    def exchange(c, off):
        peer = lax.rem(me + off, n)
        return pltpu.make_async_remote_copy(
            src_ref=stage.at[c, peer],
            dst_ref=recv.at[c, me],
            send_sem=send_sem.at[c, off],
            recv_sem=recv_sem.at[c, off],
            device_id=(peer, col),
            device_id_type=MESH,
        )

    transform(0)
    pl.semaphore_wait(barrier, 2 * n)
    for c in range(comps):
        if c > 0:
            transform(c)

        def begin(off, carry, c=c):
            exchange(c, off).start()
            return carry

        lax.fori_loop(1, n, begin, 0)

    for copy in small[2:]:
        copy.wait()
    width, starts, shifts = windows(bins)
    kinds = sorted(set(shifts))
    wide = (owners, total_slots)
    spread = jnp.where(
        lax.rem(iota((per_owner, total_slots), 1), per_owner)
        == iota((per_owner, total_slots), 0),
        1.0,
        0.0,
    )
    tiled = jnp.dot(
        slots[...].astype(f32).astype(bf16),
        spread.astype(bf16),
        preferred_element_type=f32,
    )
    own_row = iota(wide, 1) // per_owner == iota(wide, 0)
    slot_triad = jnp.sum(jnp.where(own_row, tiled, 0.0), axis=0, keepdims=True)
    holds = jnp.where(
        iota((count, total_slots), 0).astype(f32) == slot_triad, 1.0, 0.0
    ).astype(bf16)
    slot_freq = jnp.dot(
        (triads[...] + 1).astype(f32).astype(bf16), holds, preferred_element_type=f32
    )
    found = [[] for _ in kinds]
    for role in range(3):
        named = jnp.where(
            iota((K, total_slots), 0).astype(f32) + 1.0 == slot_freq[role : role + 1, :],
            1.0,
            0.0,
        )
        for side, shift in enumerate(kinds):
            spot = column.astype(f32) - float(shift)
            at_rank = jnp.where((rank == spot) & (used > 0.0), 1.0, 0.0)
            chosen_all = jnp.dot(
                at_rank.T.astype(bf16), named.astype(bf16), preferred_element_type=f32
            )
            found[side].append(chosen_all.T[:, :width])
    for side in range(len(kinds)):
        pick[side] = jnp.concatenate(
            [
                found[side][role][g * GROUP : (g + 1) * GROUP]
                for g in range(groups)
                for role in range(3)
            ],
            axis=0,
        ).astype(bf16)

    w_row = weights[pl.ds(me, 1), :] * weight_scale

    def look_up(c, src, ref):
        got = ref[c, src].astype(f32)
        for side, shift in enumerate(kinds):
            parts = [q for q in range(4) if shifts[q] == shift]
            values = [got[starts[q] : starts[q] + width] for q in parts]
            rows = jnp.dot(
                pick[side],
                jnp.concatenate(values, axis=1).astype(bf16),
                preferred_element_type=f32,
            )
            for i, q in enumerate(parts):
                looked[:, q * LANES : (q + 1) * LANES] = rows[
                    :, i * LANES : (i + 1) * LANES
                ]
        at = pl.ds(pl.multiple_of(src * 2 * GROUP, 2 * GROUP), 2 * GROUP)
        at_imag = pl.ds(
            pl.multiple_of((NB + 2 * src) * GROUP, 2 * GROUP), 2 * GROUP
        )

        def group(g, carry):
            def tile(role, q):
                row = pl.multiple_of((3 * g + role) * GROUP, GROUP)
                return looked[pl.ds(row, GROUP), q * LANES : (q + 1) * LANES]

            re, im, c_re, c_im = [], [], [], []
            for b in range(2):
                ar, ai = tile(0, 2 * b), tile(0, 2 * b + 1)
                br, bi = tile(1, 2 * b), tile(1, 2 * b + 1)
                re.append((ar * br - ai * bi) * w_row)
                im.append((ar * bi + ai * br) * w_row)
                c_re.append(tile(2, 2 * b))
                c_im.append(tile(2, 2 * b + 1))
            re, im, c_re, c_im = (
                jnp.concatenate(v, axis=0) for v in (re, im, c_re, c_im)
            )
            prod[g, at, :LANES] = re.astype(bf16)
            prod[g, at, LANES:] = im.astype(bf16)
            third[g, at, :LANES] = c_re.astype(bf16)
            third[g, at, LANES:] = c_im.astype(bf16)
            third[g, at_imag, :LANES] = c_im.astype(bf16)
            third[g, at_imag, LANES:] = (-c_re).astype(bf16)
            return carry

        lax.fori_loop(0, groups, group, 0, unroll=True)

    def gram(g):
        return lax.dot_general(
            prod[g], third[g], (((1,), (1,)), ((), ())), preferred_element_type=f32
        )

    sub = iota((GROUP, LANES), 0)
    turn = lax.rem(sub - iota((GROUP, LANES), 1) + LANES, GROUP)
    low = lax.rem(iota((NB, LANES), 1), GROUP) < GROUP // 2

    def diagonal(total, side):
        octets = []
        for o in range(NB // GROUP):
            rows = []
            for b in range(GROUP):
                at = (o * GROUP + b) * GROUP
                rows.append(total[at : at + GROUP, side * LANES : (side + 1) * LANES])
            for k in (1, 2, 4):
                even, stay = (sub & k) == 0, (turn & k) == 0
                rows = [
                    jnp.where(
                        stay,
                        jnp.where(even, rows[i], rows[i + 1]),
                        pltpu.roll(jnp.where(even, rows[i + 1], rows[i]), k, 0),
                    )
                    for i in range(0, len(rows), 2)
                ]
            octets.append(rows[0])
        return jnp.concatenate(octets, axis=0)

    def partner(step):
        total, bit = 0, 1
        while bit < n:
            total = total + lax.rem(me // bit + step // bit, 2) * bit
            bit *= 2
        return total

    half = owners // 2

    def fold(side, first, past, with_acc, with_tiles):
        def tile(at, carry):
            i, h = partner(n - 1 - side * half - at // 2), lax.rem(at, 2)
            g = i * halves + h
            total = acc[g] + gram(g) if with_acc else gram(g)
            real, imag = diagonal(total, 0), diagonal(total, 1)
            both = (
                jnp.where(low, real, pltpu.roll(imag, GROUP // 2, 1)),
                jnp.where(low, pltpu.roll(real, LANES - GROUP // 2, 1), imag),
            )
            for q in range(2):
                before = tiles[q, side, at] if with_tiles else 0.0
                tiles[q, side, at] = before + both[q]
            return carry

        lax.fori_loop(first, past, tile, 0, unroll=True)

    def finish(side, first, past):
        fold(side, first, past, False, comps > 1)

    for c in range(comps):
        look_up(c, me, stage)

        def arrive(off, carry, c=c):
            exchange(c, off).wait_recv()
            look_up(c, lax.rem(me - off + n, n), recv)
            return carry

        lax.fori_loop(1, n, arrive, 0)
        if c < comps - 2:

            def grams(g, carry, c=c):
                acc[g] = gram(g) if c == 0 else acc[g] + gram(g)
                return carry

            lax.fori_loop(0, groups, grams, 0, unroll=2)
        elif c == comps - 2:
            for side in range(2):
                fold(side, 0, n, c > 0, False)

    def swap(side):
        return pltpu.make_async_remote_copy(
            src_ref=tiles.at[1 - core, side],
            dst_ref=paired.at[side],
            send_sem=send_pair.at[side],
            recv_sem=recv_pair.at[side],
            device_id=sibling,
            device_id_type=MESH,
        )

    def deliver(side, step, h):
        return pltpu.make_async_remote_copy(
            src_ref=sums.at[side, 2 * step + h],
            dst_ref=land.at[me_at],
            send_sem=send_tile.at[side, 2 * step + h],
            recv_sem=recv_tile.at[me_at],
            device_id=(partner(n - 1 - side * half - step), 2 * h + core),
            device_id_type=MESH,
        )

    def pass_on(side):
        swap(side).wait_recv()
        chip_sum = tiles[core, side] + paired[side]
        sums[side] = chip_sum.astype(bf16)
        if side == 1:
            paired[side] = chip_sum
        for step in range(half):
            deliver(side, step, 1 - here).start()
            if side * half + step < n - 1:
                deliver(side, step, here).start()

    finish(0, 0, n)
    swap(0).start()
    finish(1, 0, 4)
    pass_on(0)
    finish(1, 4, n)
    swap(1).start()
    pass_on(1)

    def drain(off, carry):
        for c in range(comps):
            exchange(c, off).wait_send()
        return carry

    lax.fori_loop(1, n, drain, 0)
    for side in range(2):
        swap(side).wait_send()

    def landed(off):
        i, h = chip(off)
        return pltpu.make_async_remote_copy(
            src_ref=sums.at[0, 0],
            dst_ref=land.at[2 * i + h],
            send_sem=send_tile.at[0, 0],
            recv_sem=recv_tile.at[2 * i + h],
            device_id=(i, 2 * h + core),
            device_id_type=MESH,
        )

    def collect(off, carry):
        landed(off).wait_recv()
        return carry

    lax.fori_loop(1, 2 * n, collect, 0)
    total = paired[1, n - 2 + here]
    for off in range(1, 2 * n):
        total = total + land[lax.rem(me_at + off, 2 * n)].astype(f32)
    out[...] = total

    for side in range(2):
        for step in range(half):
            deliver(side, step, 1 - here).wait_send()
            if side * half + step < n - 1:
                deliver(side, step, here).wait_send()


def lean_tile(n, ns, bins, weight_scale, snap, table, weights, triads, slots):
    comps, times, cells = snap.shape
    owners, per_owner = slots.shape
    groups = owners * per_owner // GROUP
    rows = 4 * bins
    width, _, shifts = windows(bins)
    vmem = pl.BlockSpec(memory_space=pltpu.VMEM)
    anywhere = pl.BlockSpec(memory_space=pl.ANY)
    sem = pltpu.SemaphoreType.DMA
    return pl.pallas_call(
        functools.partial(lean_kernel, n, ns, bins, weight_scale),
        out_shape=jax.ShapeDtypeStruct((NB, LANES), jnp.float32),
        in_specs=[anywhere] * 5,
        out_specs=vmem,
        scratch_shapes=[
            pltpu.VMEM((comps, times, cells), jnp.bfloat16),
            pltpu.VMEM((2, K, NT), jnp.bfloat16),
            pltpu.VMEM(weights.shape, jnp.float32),
            pltpu.VMEM(triads.shape, jnp.int32),
            pltpu.VMEM(slots.shape, jnp.int32),
            pltpu.VMEM((2, -(-2 * bins // GROUP) * GROUP, NT), jnp.bfloat16),
            pltpu.VMEM((len(set(shifts)), 3 * owners * per_owner, width), jnp.bfloat16),
            pltpu.VMEM((comps, n, rows, LANES), jnp.bfloat16),
            pltpu.VMEM((comps, n, rows, LANES), jnp.bfloat16),
            pltpu.VMEM((3 * owners * per_owner, 4 * LANES), jnp.float32),
            pltpu.VMEM((groups, NB * GROUP, 2 * LANES), jnp.bfloat16),
            pltpu.VMEM((groups, 2 * NB * GROUP, 2 * LANES), jnp.bfloat16),
            pltpu.VMEM((groups, NB * GROUP, 2 * LANES), jnp.float32),
            pltpu.VMEM((2, 2, n, NB, LANES), jnp.float32),
            pltpu.VMEM((2, n, NB, LANES), jnp.float32),
            pltpu.VMEM((2, n, NB, LANES), jnp.bfloat16),
            pltpu.VMEM((2 * n, NB, LANES), jnp.bfloat16),
            sem((comps + 4,)),
            sem((comps, n)),
            sem((comps, n)),
            sem((2,)),
            sem((2,)),
            sem((2, n)),
            sem((2 * n,)),
        ],
        compiler_params=pltpu.CompilerParams(
            collective_id=bins, has_side_effects=True, vmem_limit_bytes=60 * 1024 * 1024
        ),
    )(snap, table, weights, triads, slots)


def size_class(bins, triads, out):
    count = triads.shape[1]
    freq = lax.broadcasted_iota(jnp.int32, (K, count), 0)
    hit = (
        (freq == triads[0:1, :]) | (freq == triads[1:2, :]) | (freq == triads[2:3, :])
    )
    used = jnp.sum(jnp.max(jnp.where(hit, 1.0, 0.0), axis=1, keepdims=True))
    index = jnp.int32(0)
    for size in bins[:-1]:
        index += (used > size).astype(jnp.int32)
    out[0] = index


def lean(n, ns, snapshots, cell_weights, triads, owner_slots):
    times, comps, cells = snapshots.shape
    index = pl.pallas_call(
        functools.partial(size_class, BINS),
        out_shape=jax.ShapeDtypeStruct((1,), jnp.int32),
        in_specs=[pl.BlockSpec(memory_space=pltpu.VMEM)],
        out_specs=pl.BlockSpec(memory_space=pltpu.SMEM),
    )(triads.T)
    scale = 1.0 / math.sqrt(comps * cells * ns)
    tile = lax.switch(
        index[0],
        [functools.partial(lean_tile, n, ns, bins, scale) for bins in BINS],
        snapshots.transpose(1, 0, 2),
        jnp.asarray(spectral_table().reshape(K, 2, NT).transpose(1, 0, 2)),
        cell_weights.reshape(n, LANES),
        triads.T,
        owner_slots,
    )
    mine = owner_slots.shape[1] // ns
    return tile.reshape(NB, NB, 2, mine).transpose(3, 2, 0, 1).reshape(mine, 2 * NB * NB)


def shards(n, ns, snapshots, cell_weights, triads, owner_slots):
    times, comps, cells = snapshots.shape
    owners, slot_count = owner_slots.shape
    lean_slots = ns == 4 and slot_count == 2 * GROUP and owners == n
    if lean_slots and times == 2 * NT and n & (n - 1) == 0:
        return lean(n, ns, snapshots, cell_weights, triads, owner_slots)
    weight_scale = 1.0 / math.sqrt(comps * cells * ns)
    vmem = pl.BlockSpec(memory_space=pltpu.VMEM)
    smem = pl.BlockSpec(memory_space=pltpu.SMEM)
    anywhere = pl.BlockSpec(memory_space=pl.ANY)
    sem = pltpu.SemaphoreType.DMA
    tile = pl.pallas_call(
        functools.partial(kernel, n, ns, weight_scale),
        out_shape=jax.ShapeDtypeStruct((NB, LANES), jnp.float32),
        in_specs=[anywhere, vmem, vmem, smem],
        out_specs=vmem,
        scratch_shapes=[
            pltpu.VMEM((comps, NB * NT, LANES), jnp.bfloat16),
            pltpu.VMEM((2 * K * NB, LANES), jnp.float32),
            pltpu.VMEM((K, 2 * NB, LANES), jnp.float32),
            pltpu.VMEM((K, 2 * NB, LANES), jnp.bfloat16),
            pltpu.VMEM((ns, n, NB, LANES), jnp.float32),
            pltpu.VMEM((ns - 1, n, NB, LANES), jnp.float32),
            pltpu.VMEM((n, NB, LANES), jnp.float32),
            pltpu.VMEM((n, NB, LANES), jnp.float32),
            sem((comps, n)),
            sem((comps, n)),
            sem((comps,)),
            sem((ns - 1,)),
            sem((ns - 1,)),
            sem((n,)),
            sem((n,)),
        ],
        compiler_params=pltpu.CompilerParams(
            collective_id=0, has_side_effects=True, vmem_limit_bytes=40 * 1024 * 1024
        ),
    )(
        snapshots.transpose(1, 0, 2),
        jnp.asarray(spectral_table()),
        cell_weights.reshape(n, LANES),
        jnp.take(triads.T, jnp.maximum(owner_slots, 0).reshape(-1), axis=1, mode="clip"),
    )
    mine = slot_count // ns
    flat = tile.reshape(NB, 2, mine, NB).transpose(2, 1, 0, 3).reshape(mine, 2 * NB * NB)
    my_slots = lax.dynamic_slice(
        owner_slots, (lax.axis_index("tm"), lax.axis_index("space") * mine), (1, mine)
    ).reshape(mine, 1)
    return jnp.where(my_slots >= 0, flat, 0.0)


def solution(mesh):
    placed = (P("tm", None, "space"), P("space"), P(), P())
    n, ns = mesh.shape["tm"], mesh.shape["space"]
    return jax.shard_map(
        functools.partial(shards, n, ns),
        mesh=mesh,
        in_specs=placed,
        out_specs=P(("tm", "space"), None),
        check_vma=False,
    )
```
